256 devices in a mesh: slab: 16 (over x, z_lo, core), chan: 16 (over y, z_hi).
Axes of the slice: x: 4, y: 4, z: 8 (z_hi: 4, z_lo: 2; z = z_hi * 2 + z_lo), core: 2. Of those that a mesh axis runs over, the one named last changes fastest.
Arguments:
- features: bfloat16 [64, 64, 32, 128], P('chan', 'slab'), may hold values from -6 to 6
- pre_act: bfloat16 [128, 64, 32, 128], P('chan', 'slab'), may hold values from -6 to 6
- out_grad: bfloat16 [128, 64, 32, 128], P('chan', 'slab'), may hold values from -6 to 6
- weight_one: bfloat16 [27, 64, 128], replicated, may hold values from -0.15625 to 0.15625
- weight_two: bfloat16 [27, 128, 128], replicated, may hold values from -0.109375 to 0.109375
- dropout_seed: int32 [1], replicated, may hold values from 0 to 1073741823
- layer_offset: int32 [1], replicated, may hold values from 0 to 16777215
Outputs:
- feature_grad: float32 [64, 64, 32, 128], P('chan', 'slab')
- weight_one_grad: float32 [64, 3456], P('chan')
- weight_two_grad: float32 [128, 3456], P('chan')
The draws below stay inside these ranges and needn't reach their ends.
All inputs are finite; a program needn't handle non-finite values.
Results may differ from the reference program's by a relative error of at most 0.003.
Values may be sent and summed in bfloat16 or wider, within the bound.
No kernel may reach another device: no remote copies, remote signals or barrier semaphores. Data moves between devices by JAX's collectives and lax.ppermute only.
A program may use at most 128 MiB of HBM per device.

```python
import math
import jax
import jax.numpy as jnp
from jax import lax

CIN = 64
CMID = 128
COUT = 128
NX = 128
NZ = 64
NY = 32
N_CHAN = 16


def shard_levels(stream_key, shape, shards, least, largest):
    factor_of, own = 1.0, jax.random.fold_in(stream_key, 6)
    for axis_at, blocks in shards:
        heights = jnp.exp(jax.random.uniform(jax.random.fold_in(own, axis_at), (blocks,), jnp.float32, least / len(shards), largest / len(shards)))
        factor_of = factor_of * jnp.repeat(heights, shape[axis_at] // blocks).reshape([-1 if axis == axis_at else 1 for axis in range(len(shape))])
    return factor_of


def bell_draw(rng, dims, scale, bound, shards=(), kind=jnp.bfloat16):
    result = jax.random.normal(rng, dims, jnp.float32) * scale
    if len(shards) > 0:
        result = shard_levels(rng, dims, shards, -0.22, 0.18) * result
    return jnp.clip(result, min=-bound, max=bound).astype(kind)


def setup_inputs(seed: int = 0) -> dict:
    streams_of = jax.random.split(jax.random.key(seed), 8)
    features = bell_draw(streams_of[0], (CIN, NZ, NY, NX), 1.0, 6.0, ((0, 16), (1, 16)))
    pre_act = bell_draw(streams_of[1], (CMID, NZ, NY, NX), 1.0, 6.0, ((0, 16), (1, 16)))
    out_grad = bell_draw(streams_of[2], (COUT, NZ, NY, NX), 1.0, 6.0, ((0, 16), (1, 16)))
    weight_one = bell_draw(streams_of[3], (27, CIN, CMID), (27 * CIN) ** -0.5, 0.15625)
    weight_two = bell_draw(streams_of[4], (27, CMID, COUT), (27 * CMID) ** -0.5, 0.109375)
    dropout_seed = jax.random.randint(streams_of[5], (1,), 0, 1073741824).astype(jnp.int32)
    layer_offset = jax.random.randint(streams_of[6], (1,), 0, 16777216).astype(jnp.int32)
    return dict(features=features, pre_act=pre_act, out_grad=out_grad, weight_one=weight_one, weight_two=weight_two, dropout_seed=dropout_seed, layer_offset=layer_offset)


def keep_factor(dropout_seed, layer_offset, chan_ids, depth_ids, row_ids, col_total, depth_total, row_total):
    col_ids = jnp.arange(col_total, dtype=jnp.int32)
    position = ((chan_ids[:, None, None, None] * depth_total + depth_ids[None, :, None, None]) * row_total + row_ids[None, None, :, None]) * col_total + col_ids[None, None, None, :]
    hashed = position + layer_offset[0] ^ dropout_seed[0]
    hashed = hashed * 739982445
    hashed = hashed ^ lax.shift_right_logical(hashed, jnp.int32(15))
    hashed = hashed * 695938361
    hashed = hashed ^ lax.shift_right_logical(hashed, jnp.int32(12))
    kept = hashed & 65535 < 52429
    return jnp.where(kept, 1.25, 0.0).astype(jnp.float32)

def tap_columns(source, depth_len, row_len, col_len):
    pieces = []
    for depth_tap in range(3):
        for row_tap in range(3):
            for col_tap in range(3):
                pieces.append(source[:, 2 - depth_tap:2 - depth_tap + depth_len, 2 - row_tap:2 - row_tap + row_len, 2 - col_tap:2 - col_tap + col_len])
    stacked = jnp.stack(pieces, axis=0)
    return stacked.reshape(27 * source.shape[0], depth_len * row_len * col_len)

def tap_lhs(weight):
    return weight.transpose(1, 2, 0).reshape(weight.shape[1], 27 * weight.shape[0])

def weight_grad(columns, activation, group_n):
    product = lax.dot_general(columns, activation.reshape(activation.shape[0], -1), (((1,), (1,)), ((), ())), preferred_element_type=jnp.float32)
    return product.reshape(27, group_n, activation.shape[0]).transpose(1, 2, 0)

def grouped_weight_grad(grad_zero, activation, depth_len, row_len, col_len, group_count):
    group_n = grad_zero.shape[0] // group_count

    def one_group(group_pos):
        grad_part = lax.dynamic_slice_in_dim(grad_zero, group_pos * group_n, group_n, 0)
        return weight_grad(tap_columns(grad_part, depth_len, row_len, col_len), activation, group_n)
    blocks = lax.map(one_group, jnp.arange(group_count, dtype=jnp.int32))
    return blocks.reshape(group_count * group_n, activation.shape[0], 27)

def grouped_input_grad(grad_pad, weight, depth_len, row_len, col_len, group_count):
    group_n = grad_pad.shape[0] // group_count

    def add_group(running, group_pos):
        grad_part = lax.dynamic_slice_in_dim(grad_pad, group_pos * group_n, group_n, 0)
        lhs_part = tap_lhs(lax.dynamic_slice_in_dim(weight, group_pos * group_n, group_n, 0))
        term = jnp.dot(lhs_part, tap_columns(grad_part, depth_len, row_len, col_len), preferred_element_type=jnp.float32)
        return (running + term, None)
    start_total = jnp.zeros((weight.shape[1], depth_len * row_len * col_len), jnp.float32)
    running, unused = lax.scan(add_group, start_total, jnp.arange(group_count, dtype=jnp.int32))
    return running.reshape(weight.shape[1], depth_len, row_len, col_len)

def reference(features, pre_act, out_grad, weight_one, weight_two, dropout_seed, layer_offset):
    filters_one = weight_one.transpose(2, 1, 0)
    filters_two = weight_two.transpose(2, 1, 0)
    kept_scale = keep_factor(dropout_seed, layer_offset, jnp.arange(CMID, dtype=jnp.int32), jnp.arange(NZ, dtype=jnp.int32), jnp.arange(NY, dtype=jnp.int32), NX, NZ, NY)
    hidden_act = (jnp.maximum(pre_act.astype(jnp.float32), 0.0) * kept_scale).astype(jnp.bfloat16)
    grad_scale = 1.0 / math.sqrt(NZ * NY * NX)
    act_ext = jnp.pad(hidden_act, ((0, 0), (1, 1), (1, 1), (0, 0)))
    grad_zero = jnp.pad(out_grad, ((0, 0), (2, 2), (2, 2), (1, 1)))
    raw_two = grouped_weight_grad(grad_zero, act_ext, NZ + 2, NY + 2, NX, N_CHAN)
    grad_pad = jnp.pad(out_grad, ((0, 0), (1, 1), (1, 1), (1, 1)))
    hidden_grad = grouped_input_grad(grad_pad, filters_two, NZ, NY, NX, N_CHAN)
    pre_grad = jnp.where(pre_act > 0, hidden_grad * kept_scale, 0.0).astype(jnp.bfloat16)
    feat_ext = jnp.pad(features, ((0, 0), (1, 1), (1, 1), (0, 0)))
    pre_zero = jnp.pad(pre_grad, ((0, 0), (2, 2), (2, 2), (1, 1)))
    raw_one = grouped_weight_grad(pre_zero, feat_ext, NZ + 2, NY + 2, NX, N_CHAN)
    pre_pad = jnp.pad(pre_grad, ((0, 0), (1, 1), (1, 1), (1, 1)))
    feature_grad = grouped_input_grad(pre_pad, filters_one, NZ, NY, NX, N_CHAN)
    one_out = (raw_one * grad_scale).reshape(CMID // 2, 54 * CIN)
    two_out = (raw_two * grad_scale).reshape(COUT, 27 * CMID)
    return (feature_grad, one_out, two_out)
```

```python
import math

import jax
import jax.numpy as jnp
from jax import lax
from jax.experimental import pallas as pl
from jax.experimental.pallas import tpu as pltpu
from jax.sharding import Mesh
from jax.sharding import PartitionSpec as P

BF16, F32 = jnp.bfloat16, jnp.float32
CHAN, SLAB = ("y", "zh"), ("x", "zl", "core")
Z, R, X = 4, 2, 128
NZ, NY = 64, 32
MID, CIN = 128, 64


def kept_scale(offset, seed, z, h, shape):
    c = lax.broadcasted_iota(jnp.int32, shape, 0)
    w = lax.broadcasted_iota(jnp.int32, shape, 1)
    position = ((c * NZ + z) * NY + h) * X + w
    m = (position + offset) ^ seed
    m = m * jnp.int32(739982445)
    m = m ^ lax.shift_right_logical(m, jnp.int32(15))
    m = m * jnp.int32(695938361)
    m = m ^ lax.shift_right_logical(m, jnp.int32(12))
    return jnp.where((m & 65535) < 52429, F32(1.25), F32(0.0))


def store_shifts(dst, plane, row, block):
    n = block.shape[0]
    lane = lax.broadcasted_iota(jnp.int32, block.shape, 1)
    cols = slice(row * X, (row + 1) * X)
    ahead = jnp.where(lane == X - 1, 0.0, pltpu.roll(block, X - 1, 1))
    behind = jnp.where(lane == 0, 0.0, pltpu.roll(block, 1, 1))
    dst[plane, 0:n, cols] = ahead.astype(BF16)
    dst[plane, n : 2 * n, cols] = block.astype(BF16)
    dst[plane, 2 * n : 3 * n, cols] = behind.astype(BF16)


def dot(a, b):
    return lax.dot_general(a, b, (((1,), (0,)), ((), ())), preferred_element_type=F32)


def dot_t(a, b):
    return lax.dot_general(a, b, (((1,), (1,)), ((), ())), preferred_element_type=F32)


def kernel(scal, own, left, right, feat, w_two, w_one, wout, fout, g3, p3, act, hid, fin):
    z0, h0, offset, seed = scal[0], scal[1], scal[2], scal[3]

    def build(src, base, at):
        def step(i, _):
            for row in range(6):
                store_shifts(g3, at + i, row, src[base + i * 6 + row].astype(F32))
            return 0

        return step

    lax.fori_loop(0, 2, build(left, 0, 0), 0)
    lax.fori_loop(0, 4, build(own, 0, 2), 0)
    lax.fori_loop(0, 2, build(right, 0, 6), 0)

    hid[...] = jnp.zeros_like(hid)

    def spread(i, _):
        for kd in range(3):
            total = None
            for kh in range(3):
                q = kd * 3 + kh
                lhs = jnp.concatenate([w_two[3 * q], w_two[3 * q + 1], w_two[3 * q + 2]], axis=1)
                part = dot(lhs, g3[i, :, (2 - kh) * X : (6 - kh) * X])
                total = part if total is None else total + part
            hid[i + kd] = hid[i + kd] + total
        return 0

    lax.fori_loop(0, 8, spread, 0)

    def mask(j, pre_of):
        for row in range(4):
            scale = kept_scale(offset, seed, z0 - 1 + j, h0 - 1 + row, (MID, X))
            pre = pre_of(row).astype(F32)
            grad = hid[j + 2, :, row * X : (row + 1) * X]
            store_shifts(p3, j, row, jnp.where(pre > 0, grad * scale, 0.0))
            yield row, pre, scale

    for _ in mask(0, lambda row: left[12 + row]):
        pass
    for _ in mask(5, lambda row: right[12 + row]):
        pass

    def inner(i, _):
        for row, pre, scale in mask(i + 1, lambda row: own[24 + i * 4 + row]):
            if row in (1, 2):
                act[i, :, (row - 1) * X : row * X] = (jnp.maximum(pre, 0.0) * scale).astype(BF16)
        return 0

    lax.fori_loop(0, Z, inner, 0)

    for q in range(9):
        kd, kh = divmod(q, 3)
        total = None
        for i in range(Z):
            rows = g3[i + 3 - kd, :, (3 - kh) * X : (5 - kh) * X]
            part = dot_t(rows, act[i])
            total = part if total is None else total + part
        for kw in range(3):
            wout[3 * q + kw] = total[kw * 128 : (kw + 1) * 128]

    blank = jnp.zeros((CIN, R * X), BF16)
    for q in range(5):
        total = None
        for i in range(Z):
            f = feat[i]
            for tap, rhs in ((q, jnp.concatenate([f, blank], 0)), (q + 5, jnp.concatenate([blank, f], 0))):
                if tap > 8:
                    continue
                kd, kh = divmod(tap, 3)
                part = dot_t(p3[i + 2 - kd, :, (2 - kh) * X : (4 - kh) * X], rhs)
                total = part if total is None else total + part
        for kw in range(3):
            wout[27 + 3 * q + kw] = total[kw * 128 : (kw + 1) * 128]

    fin[...] = jnp.zeros_like(fin)

    def spread_one(i, _):
        for kd in range(3):
            total = None
            for kh in range(3):
                q = kd * 3 + kh
                lhs = jnp.concatenate([w_one[3 * q], w_one[3 * q + 1], w_one[3 * q + 2]], axis=1)
                part = dot(lhs, p3[i, :, (2 - kh) * X : (4 - kh) * X])
                total = part if total is None else total + part
            fin[i + kd] = fin[i + kd] + total
        return 0

    lax.fori_loop(0, 6, spread_one, 0)
    for i in range(Z):
        fout[i] = fin[i + 2].astype(BF16)


def on_cells(scal, own, left, right, feat, weight_two, weight_one):
    vmem = pl.BlockSpec(memory_space=pltpu.VMEM)
    return pl.pallas_call(
        kernel,
        out_shape=(
            jax.ShapeDtypeStruct((42, 128, 128), F32),
            jax.ShapeDtypeStruct((Z, CIN, R * X), BF16),
        ),
        in_specs=[pl.BlockSpec(memory_space=pltpu.SMEM)] + [vmem] * 6,
        out_specs=(vmem, vmem),
        scratch_shapes=[
            pltpu.VMEM((8, 384, 6 * X), BF16),
            pltpu.VMEM((6, 384, 4 * X), BF16),
            pltpu.VMEM((Z, MID, R * X), BF16),
            pltpu.VMEM((10, MID, 4 * X), F32),
            pltpu.VMEM((8, CIN, R * X), F32),
        ],
        compiler_params=pltpu.CompilerParams(vmem_limit_bytes=48 * 1024 * 1024),
    )(scal, own, left, right, feat, weight_two, weight_one)


def shards(features, pre_act, out_grad, weight_one, weight_two, dropout_seed, layer_offset):
    chan_pos, slab_pos = lax.axis_index(CHAN), lax.axis_index(SLAB)
    core = lax.axis_index("core")

    grad = jnp.pad(out_grad.transpose(1, 2, 0, 3), ((0, 0), (2, 2), (0, 0), (0, 0))).reshape(Z, 18, 2, 8, X)
    grad = jnp.stack([grad[:, i : i + 16] for i in range(3)], axis=2)
    grad = grad.transpose(1, 0, 2, 3, 4, 5).reshape(16, 24, 8, X)
    pre = jnp.pad(pre_act.transpose(1, 2, 0, 3), ((0, 0), (1, 1), (0, 0), (0, 0))).reshape(Z, 17, 2, 8, X)
    pre = jnp.stack([pre[:, i : i + 16] for i in range(2)], axis=2)
    pre = pre.transpose(1, 0, 2, 3, 4, 5).reshape(16, 16, 8, X)
    feat = features.reshape(4, Z, 16, R, X).transpose(2, 1, 3, 0, 4).reshape(16, Z, 8, X)
    sent = jnp.concatenate([grad, pre, feat], axis=1)
    got = lax.all_to_all(sent, CHAN, 0, 0, tiled=True)
    cells = got.transpose(1, 0, 2, 3).reshape(44, 128, X)
    own = cells[:40]
    feat = cells[40:].reshape(Z, 16, R, 4, X).transpose(0, 1, 3, 2, 4).reshape(Z, CIN, R * X)

    up = [(i, i + 1) for i in range(15)]
    down = [(i + 1, i) for i in range(15)]
    left = lax.ppermute(jnp.concatenate([own[12:24], own[36:40]]), SLAB, up)
    right = lax.ppermute(jnp.concatenate([own[0:12], own[24:28]]), SLAB, down)

    scal = jnp.stack([slab_pos * Z, chan_pos * R, layer_offset[0], dropout_seed[0]])
    filters, feature = on_cells(scal, own, left, right, feat, weight_two, weight_one)

    filters = filters.reshape(2, 21, 128, 128)
    theirs = lax.dynamic_index_in_dim(filters, 1 - core, 0, keepdims=False).astype(BF16)
    mine = lax.dynamic_index_in_dim(filters, core, 0, keepdims=False)
    mine = mine + lax.ppermute(theirs, "core", [(0, 1), (1, 0)]).astype(F32)
    mine = mine.astype(BF16).reshape(21, 16, 8, 128).transpose(1, 0, 2, 3)
    feature = feature.reshape(Z, 16, 4, R, X).transpose(1, 0, 3, 2, 4).reshape(16, Z, 8, X)
    got = lax.all_to_all(jnp.concatenate([mine, feature], axis=1), CHAN, 0, 0, tiled=True)
    feature = got[:, 21:].reshape(16, Z, R, 4, X).transpose(3, 1, 0, 2, 4).reshape(4, Z, NY, X).astype(F32)
    part = got[:, :21].astype(F32).sum(axis=0)
    copies = jnp.broadcast_to(part[None], (8, 21, 8, 128))
    part = lax.all_to_all(copies, ("x", "zl"), 0, 0, tiled=True).sum(axis=0)
    scale = 1.0 / math.sqrt(NZ * NY * X)
    total = lax.all_gather(part * scale, "core", axis=0, tiled=True)
    two = total[:27].transpose(1, 2, 0).reshape(8, 27 * MID)
    one = total[27:].reshape(5, 3, 8, 2, CIN).transpose(3, 0, 1, 2, 4).reshape(30, 8, CIN)[:27]
    one = one.transpose(1, 2, 0).reshape(4, 54 * CIN)
    return feature, one, two


def solution(mesh):
    split = Mesh(mesh.devices.reshape(4, 2, 2, 4, 4), ("x", "zl", "core", "y", "zh"))
    cells = P(CHAN, SLAB, None, None)
    return jax.shard_map(
        shards,
        mesh=split,
        in_specs=(cells, cells, cells, P(), P(), P(), P()),
        out_specs=(cells, P(CHAN, None), P(CHAN, None)),
        check_vma=False,
    )
```

```python
import math

import jax
import jax.numpy as jnp
from jax import lax
from jax.experimental import pallas as pl
from jax.experimental.pallas import tpu as pltpu
from jax.sharding import Mesh
from jax.sharding import PartitionSpec as P

BF16, F32 = jnp.bfloat16, jnp.float32
CHAN, SLAB = ("y", "zh"), ("x", "zl", "core")
Z, R, X = 4, 2, 128
NZ, NY = 64, 32
MID, CIN = 128, 64
TILES = 8


def kept_scale(offset, seed, z, h):
    c = lax.broadcasted_iota(jnp.int32, (MID, X), 0)
    w = lax.broadcasted_iota(jnp.int32, (MID, X), 1)
    position = ((c * NZ + z) * NY + h) * X + w
    m = (position + offset) ^ seed
    m = m * jnp.int32(739982445)
    m = m ^ lax.shift_right_logical(m, jnp.int32(15))
    m = m * jnp.int32(695938361)
    m = m ^ lax.shift_right_logical(m, jnp.int32(12))
    return jnp.where((m & 65535) < 52429, F32(1.25), F32(0.0))


def store_shifts(dst, plane, row, block):
    lane = lax.broadcasted_iota(jnp.int32, block.shape, 1)
    cols = slice(row * X, (row + 1) * X)
    ahead = jnp.where(lane == X - 1, 0.0, pltpu.roll(block, X - 1, 1))
    behind = jnp.where(lane == 0, 0.0, pltpu.roll(block, 1, 1))
    dst[plane, 0:128, cols] = ahead.astype(BF16)
    dst[plane, 128:256, cols] = block.astype(BF16)
    dst[plane, 256:384, cols] = behind.astype(BF16)


def dot(a, b):
    return lax.dot_general(a, b, (((1,), (0,)), ((), ())), preferred_element_type=F32)


def dot_t(a, b):
    return lax.dot_general(a, b, (((1,), (1,)), ((), ())), preferred_element_type=F32)


def tile(ref, t):
    return ref[:, t].astype(F32).reshape(128, X)


def store_halves(core, mine, theirs, s, step, slab):
    for me in range(2):

        @pl.when(core == me)
        def _():
            for half in range(2):
                if 0 <= s - half * step <= step:
                    if half == me:
                        mine[s - half * step] = slab
                    else:
                        theirs[s - half * step] = slab.astype(BF16)


def kernel_a(got, w_two, g3, own, left, right, wk):
    for kd in range(3):
        for kh in range(3):
            for kw in range(3):
                wk[kh, kd * MID : (kd + 1) * MID, kw * 128 : (kw + 1) * 128] = w_two[9 * kd + 3 * kh + kw]
    for z in range(Z):
        for r in range(4):
            store_shifts(g3, z, r, tile(got, z * TILES + r))
    own[...] = jnp.zeros_like(own)
    for z in range(Z):
        total = None
        for kh in range(3):
            part = dot(wk[kh], g3[z, :, (2 - kh) * X : (4 - kh) * X])
            total = part if total is None else total + part
        for kd in range(3):
            term = total[kd * MID : (kd + 1) * MID]
            target = z + kd - 1
            if target < 0:
                left[...] = term
            elif target == Z:
                right[...] = term
            else:
                own[target] = own[target] + term


def kernel_b(scal, got, halo_l, halo_r, g3, mask, mine, theirs, act):
    z0, h0, offset, seed, core = scal[0], scal[1], scal[2], scal[3], scal[4]
    for w in range(-1, Z + 1):
        for r in range(R):
            ref, t = (halo_l, r) if w < 0 else (halo_r, r) if w == Z else (got, w * TILES + 4 + r)
            pre = tile(ref, t)
            if w < 0:
                pre = jnp.where(scal[5] > 0, pre, 0.0)
            elif w == Z:
                pre = jnp.where(scal[6] > 0, pre, 0.0)
            scale = kept_scale(offset, seed, z0 + w, h0 + r)
            act[w + 1, :, r * X : (r + 1) * X] = (jnp.maximum(pre, 0.0) * scale).astype(BF16)
            if 0 <= w < Z:
                mask[w, :, r * X : (r + 1) * X] = jnp.where(pre > 0, scale, 0.0).astype(BF16)
    for q in range(9):
        kd, kh = divmod(q, 3)
        total = None
        for s in range(Z):
            part = dot_t(g3[s, :, (2 - kh) * X : (4 - kh) * X], act[s + kd])
            total = part if total is None else total + part
        for kw in range(3):
            store_halves(core, mine, theirs, 3 * q + kw, 13, total[kw * 128 : (kw + 1) * 128])


def shuffle(back):
    i = lax.broadcasted_iota(jnp.int32, (128, 128), 1 if back else 0)
    j = lax.broadcasted_iota(jnp.int32, (128, 128), 0 if back else 1)
    at = (lax.rem(i, 64) // 4) * 8 + (i // 64) * 4 + lax.rem(i, 4)
    return jnp.where(at == j, F32(1.0), F32(0.0)).astype(BF16)


def kernel_c(scal, hid, from_l, from_r, mask, w_one, p3, fout, fl, fr, wk, fin):
    for kd in range(3):
        for kh in range(3):
            for kw in range(3):
                at = (kh * 3 + kd) * CIN
                wk[at : at + CIN, kw * 128 : (kw + 1) * 128] = w_one[9 * kd + 3 * kh + kw]
    for z in range(Z):
        grad = hid[z]
        if z == 0:
            grad = grad + jnp.where(scal[5] > 0, from_l[...], 0.0)
        if z == Z - 1:
            grad = grad + jnp.where(scal[6] > 0, from_r[...], 0.0)
        grad = grad * mask[z].astype(F32)
        for r in range(R):
            store_shifts(p3, z, r, grad[:, r * X : (r + 1) * X])
    fin[...] = jnp.zeros_like(fin)
    for s in range(Z):
        terms = dot(wk[...], p3[s])
        for kd in range(3):
            for kh in range(3):
                at = (kh * 3 + kd) * CIN
                cols = slice(kh * X, (kh + 2) * X)
                fin[s + kd, :, cols] = fin[s + kd, :, cols] + terms[at : at + CIN]
    back = shuffle(True)
    for w in range(-1, Z + 1):
        for i in range(2):
            rows = jnp.concatenate([fin[w + 1, :, (2 * i + r) * X : (2 * i + r + 1) * X] for r in range(2)], axis=0)
            high = rows.astype(BF16)
            tiles = dot(back, high)
            if w < 0:
                fl[:, i] = tiles.reshape(16, 8, X).astype(BF16)
            elif w == Z:
                fr[:, i] = tiles.reshape(16, 8, X).astype(BF16)
            else:
                tiles = tiles + dot(back, (rows - high.astype(F32)).astype(BF16))
                fout[:, 2 * w + i] = tiles.reshape(16, 8, X)


def kernel_d(scal, got, halo_l, halo_r, p3, mine, theirs, lo, hi):
    core = scal[4]
    lo[...] = jnp.zeros_like(lo)
    hi[...] = jnp.zeros_like(hi)
    order = shuffle(False)
    for w in range(-1, Z + 1):
        for i in range(2):
            ref, t = (halo_l, 2 + i) if w < 0 else (halo_r, 2 + i) if w == Z else (got, w * TILES + 6 + i)
            rows = dot(order, tile(ref, t).astype(BF16))
            if w < 0:
                rows = jnp.where(scal[5] > 0, rows, 0.0)
            elif w == Z:
                rows = jnp.where(scal[6] > 0, rows, 0.0)
            rows = rows.astype(BF16)
            for r in range(2):
                cols = slice((2 * i + r) * X, (2 * i + r + 1) * X)
                lo[w + 1, 0:CIN, cols] = rows[r * CIN : (r + 1) * CIN]
                hi[w + 1, CIN:, cols] = rows[r * CIN : (r + 1) * CIN]
    for q in range(5):
        total = None
        for s in range(Z):
            for tap, rhs in ((q, lo), (q + 5, hi)):
                if tap > 8:
                    continue
                kd, kh = divmod(tap, 3)
                part = dot_t(p3[s], rhs[s + kd, :, kh * X : (kh + 2) * X])
                total = part if total is None else total + part
        for kw in range(3):
            store_halves(core, mine, theirs, 3 * q + kw, 7, total[kw * 128 : (kw + 1) * 128])


VMEM, SMEM = pl.BlockSpec(memory_space=pltpu.VMEM), pl.BlockSpec(memory_space=pltpu.SMEM)


def call(body, args, outs, scratch, flops, scalars):
    return pl.pallas_call(
        body,
        out_shape=tuple(jax.ShapeDtypeStruct(shape, kind) for shape, kind in outs),
        in_specs=[SMEM] * scalars + [VMEM] * (len(args) - scalars),
        out_specs=(VMEM,) * len(outs),
        scratch_shapes=[pltpu.VMEM(shape, kind) for shape, kind in scratch],
        compiler_params=pltpu.CompilerParams(vmem_limit_bytes=24 * 1024 * 1024),
        cost_estimate=pl.CostEstimate(flops=flops, bytes_accessed=4 * 1024 * 1024, transcendentals=0),
    )(*args)


def pairs(rows, count, width):
    return jnp.stack([rows[:, i : i + 16] for i in range(count)], axis=2).swapaxes(0, 1).reshape(16, Z, width, 8, X)


def shards(features, pre_act, out_grad, weight_one, weight_two, dropout_seed, layer_offset):
    chan_pos, slab_pos, core = lax.axis_index(CHAN), lax.axis_index(SLAB), lax.axis_index("core")
    edge = ((0, 0), (1, 1), (0, 0), (0, 0))

    grad = jnp.pad(out_grad.transpose(1, 2, 0, 3), edge).reshape(Z, 17, 2, 8, X)
    pre = pre_act.transpose(1, 2, 0, 3).reshape(Z, 16, 2, 8, X)
    feat = jnp.pad(features.transpose(1, 2, 0, 3), edge).reshape(Z, 17, 1, 8, X)
    sent = jnp.concatenate([pairs(grad, 2, 4), pairs(pre, 1, 2), pairs(feat, 2, 2)], axis=2)
    got = lax.all_to_all(sent.reshape(16, Z * TILES, 8, X), CHAN, 0, 0, tiled=True)

    up = [(i, (i + 1) % 16) for i in range(16)]
    down = [((i + 1) % 16, i) for i in range(16)]
    has_l, has_r = slab_pos > 0, slab_pos < 15
    swap = [(0, 1), (1, 0)]
    halo_l = lax.ppermute(got[:, 3 * TILES + 4 :], SLAB, up)
    halo_r = lax.ppermute(got[:, 4:TILES], SLAB, down)
    scal = jnp.stack(
        [slab_pos * Z, chan_pos * R, layer_offset[0], dropout_seed[0], core, has_l.astype(jnp.int32), has_r.astype(jnp.int32)]
    )

    g3, hid, left, right = call(
        kernel_a,
        (got, weight_two),
        [((Z, 384, 4 * X), BF16), ((Z, MID, R * X), F32), ((MID, R * X), F32), ((MID, R * X), F32)],
        [((3, 384, 384), BF16)],
        10**9,
        0,
    )
    from_l = lax.ppermute(right, SLAB, up)
    from_r = lax.ppermute(left, SLAB, down)
    mask, mine_two, theirs_two = call(
        kernel_b,
        (scal, got, halo_l, halo_r, g3),
        [((Z, MID, R * X), BF16), ((14, 128, 128), F32), ((14, 128, 128), BF16)],
        [((Z + 2, MID, R * X), BF16)],
        4 * 10**9,
        1,
    )
    p3, feature, feature_l, feature_r = call(
        kernel_c,
        (scal, hid, from_l, from_r, mask, weight_one),
        [((Z, 384, R * X), BF16), ((16, 8, 8, X), F32), ((16, 2, 8, X), BF16), ((16, 2, 8, X), BF16)],
        [((9 * CIN, 384), BF16), ((Z + 2, CIN, 4 * X), F32)],
        2 * 10**9,
        1,
    )
    mine_one, theirs_one = call(
        kernel_d,
        (scal, got, halo_l, halo_r, p3),
        [((8, 128, 128), F32), ((8, 128, 128), BF16)],
        [((Z + 2, 128, 4 * X), BF16), ((Z + 2, 128, 4 * X), BF16)],
        2 * 10**9,
        1,
    )

    mine_two = mine_two + lax.ppermute(theirs_two, "core", swap).astype(F32)
    mine_one = mine_one + lax.ppermute(theirs_one, "core", swap).astype(F32)
    mine = jnp.concatenate([mine_two, mine_one]).astype(BF16).reshape(22, 16, 8, 128).transpose(1, 0, 2, 3)
    feature_l, feature_r = (
        jnp.where(has_l, lax.ppermute(feature_r, SLAB, up).astype(F32), 0.0),
        jnp.where(has_r, lax.ppermute(feature_l, SLAB, down).astype(F32), 0.0),
    )
    feature = jnp.concatenate(
        [feature[:, 0:2] + feature_l, feature[:, 2:6], feature[:, 6:8] + feature_r], axis=1
    ).astype(BF16)
    got = lax.all_to_all(jnp.concatenate([mine, feature], axis=1), CHAN, 0, 0, tiled=True)

    rows = got[:, 22:].astype(F32).reshape(16, Z, 4, 4, X)
    none = jnp.zeros((1, Z, 4, X), F32)
    first = rows[:, :, 1] + jnp.concatenate([none, rows[:-1, :, 3]])
    second = rows[:, :, 2] + jnp.concatenate([rows[1:, :, 0], none])
    feature = jnp.stack([first, second], axis=2).transpose(3, 1, 0, 2, 4).reshape(4, Z, NY, X)

    part = got[:, :22].astype(F32).sum(axis=0)
    part = part + lax.ppermute(part, "zl", swap)
    part = part + lax.ppermute(part, "x", [(i, i ^ 1) for i in range(4)])
    part = part + lax.ppermute(part, "x", [(i, i ^ 2) for i in range(4)])
    scale = 1.0 / math.sqrt(NZ * NY * X)
    total = lax.all_gather(part * scale, "core", axis=0, tiled=False)
    two = jnp.concatenate([total[0, :14], total[1, 1:14]])
    one = jnp.concatenate([total[0, 14:], total[1, 15:]])
    two = two.transpose(1, 2, 0).reshape(8, 27 * MID)
    one = one.reshape(5, 3, 8, 2, CIN).transpose(3, 0, 1, 2, 4).reshape(30, 8, CIN)[:27]
    one = one.transpose(1, 2, 0).reshape(4, 54 * CIN)
    return feature, one, two


def solution(mesh):
    split = Mesh(mesh.devices.reshape(4, 2, 2, 4, 4), ("x", "zl", "core", "y", "zh"))
    cells = P(CHAN, SLAB, None, None)
    return jax.shard_map(
        shards,
        mesh=split,
        in_specs=(cells, cells, cells, P(), P(), P(), P()),
        out_specs=(cells, P(CHAN, None), P(CHAN, None)),
        check_vma=False,
    )
```

```python
import math

import jax
import jax.numpy as jnp
from jax import lax
from jax.experimental import pallas as pl
from jax.experimental.pallas import tpu as pltpu
from jax.sharding import Mesh
from jax.sharding import PartitionSpec as P

BF16, F32 = jnp.bfloat16, jnp.float32
CHAN, SLAB = ("y", "zh"), ("x", "zl", "core")
Z, R, X = 4, 2, 128
NZ, NY = 64, 32
MID, CIN = 128, 64
TILES = 8


def kept_scale(offset, seed, z, h):
    c = lax.broadcasted_iota(jnp.int32, (MID, X), 0)
    w = lax.broadcasted_iota(jnp.int32, (MID, X), 1)
    position = ((c * NZ + z) * NY + h) * X + w
    m = (position + offset) ^ seed
    m = m * jnp.int32(739982445)
    m = m ^ lax.shift_right_logical(m, jnp.int32(15))
    m = m * jnp.int32(695938361)
    m = m ^ lax.shift_right_logical(m, jnp.int32(12))
    return jnp.where((m & 65535) < 52429, F32(1.25), F32(0.0))


def store_shifts(dst, plane, row, block):
    lane = lax.broadcasted_iota(jnp.int32, block.shape, 1)
    cols = slice(row * X, (row + 1) * X)
    ahead = jnp.where(lane == X - 1, 0.0, pltpu.roll(block, X - 1, 1))
    behind = jnp.where(lane == 0, 0.0, pltpu.roll(block, 1, 1))
    dst[plane, 0:128, cols] = ahead.astype(BF16)
    dst[plane, 128:256, cols] = block.astype(BF16)
    dst[plane, 256:384, cols] = behind.astype(BF16)


def dot(a, b):
    return lax.dot_general(a, b, (((1,), (0,)), ((), ())), preferred_element_type=F32)


def dot_t(a, b):
    return lax.dot_general(a, b, (((1,), (1,)), ((), ())), preferred_element_type=F32)


def tile(ref, t):
    return ref[:, t].astype(F32).reshape(128, X)


def store_halves(core, mine, theirs, s, count, step, slab):
    for me in range(2):

        @pl.when(core == me)
        def _():
            for half in range(2):
                if 0 <= s - half * step < count:
                    dst = mine if half == me else theirs
                    dst[s - half * step] = slab.astype(dst.dtype)


def kernel_a(got, w_two, g3, own, left, right, wk):
    for kd in range(3):
        for kh in range(3):
            for kw in range(3):
                wk[kh, kd * MID : (kd + 1) * MID, kw * 128 : (kw + 1) * 128] = w_two[9 * kd + 3 * kh + kw]
    for z in range(Z):
        for r in range(4):
            store_shifts(g3, z, r, tile(got, z * TILES + r))
    own[...] = jnp.zeros_like(own)
    for z in range(Z):
        total = None
        for kh in range(3):
            part = dot(wk[kh], g3[z, :, (2 - kh) * X : (4 - kh) * X])
            total = part if total is None else total + part
        for kd in range(3):
            term = total[kd * MID : (kd + 1) * MID]
            target = z + kd - 1
            if target < 0:
                left[...] = term
            elif target == Z:
                right[...] = term
            else:
                own[target] = own[target] + term


def kernel_b(scal, got, halo_l, halo_r, g3, mask, mine, theirs, act):
    z0, h0, offset, seed, core = scal[0], scal[1], scal[2], scal[3], scal[4]
    for w in range(-1, Z + 1):
        for r in range(R):
            ref, t = (halo_l, r) if w < 0 else (halo_r, r) if w == Z else (got, w * TILES + 4 + r)
            pre = tile(ref, t)
            if w < 0:
                pre = jnp.where(scal[5] > 0, pre, 0.0)
            elif w == Z:
                pre = jnp.where(scal[6] > 0, pre, 0.0)
            scale = kept_scale(offset, seed, z0 + w, h0 + r)
            cols = slice(r * X, (r + 1) * X)
            act[(w + 1) * MID : (w + 2) * MID, cols] = (jnp.maximum(pre, 0.0) * scale).astype(BF16)
            if 0 <= w < Z:
                mask[w, :, cols] = jnp.where(pre > 0, scale, 0.0).astype(BF16)
    for kh in range(3):
        total = None
        for s in range(Z):
            part = dot_t(g3[s, :, (2 - kh) * X : (4 - kh) * X], act[s * MID : (s + 3) * MID])
            total = part if total is None else total + part
        for kd in range(3):
            for kw in range(3):
                slab = total[kw * 128 : (kw + 1) * 128, kd * MID : (kd + 1) * MID]
                store_halves(core, mine, theirs, 9 * kd + 3 * kh + kw, 14, 13, slab)


def shuffle(back):
    i = lax.broadcasted_iota(jnp.int32, (128, 128), 1 if back else 0)
    j = lax.broadcasted_iota(jnp.int32, (128, 128), 0 if back else 1)
    at = (lax.rem(i, 64) // 4) * 8 + (i // 64) * 4 + lax.rem(i, 4)
    return jnp.where(at == j, F32(1.0), F32(0.0)).astype(BF16)


def kernel_c(scal, hid, from_l, from_r, mask, w_one, p3, fout, fl, fr, wk, fin):
    for kd in range(3):
        for kh in range(3):
            for kw in range(3):
                at = (kh * 3 + kd) * CIN
                wk[at : at + CIN, kw * 128 : (kw + 1) * 128] = w_one[9 * kd + 3 * kh + kw]
    for z in range(Z):
        grad = hid[z]
        if z == 0:
            grad = grad + jnp.where(scal[5] > 0, from_l[...], 0.0)
        if z == Z - 1:
            grad = grad + jnp.where(scal[6] > 0, from_r[...], 0.0)
        grad = grad * mask[z].astype(F32)
        for r in range(R):
            store_shifts(p3, z, r, grad[:, r * X : (r + 1) * X])
    fin[...] = jnp.zeros_like(fin)
    for s in range(Z):
        terms = dot(wk[...], p3[s])
        for kd in range(3):
            for kh in range(3):
                at = (kh * 3 + kd) * CIN
                cols = slice(kh * X, (kh + 2) * X)
                fin[s + kd, :, cols] = fin[s + kd, :, cols] + terms[at : at + CIN]
    back = shuffle(True)
    for w in range(-1, Z + 1):
        for i in range(2):
            rows = jnp.concatenate([fin[w + 1, :, (2 * i + r) * X : (2 * i + r + 1) * X] for r in range(2)], axis=0)
            high = rows.astype(BF16)
            tiles = dot(back, high)
            if w < 0:
                fl[:, i] = tiles.reshape(16, 8, X).astype(BF16)
            elif w == Z:
                fr[:, i] = tiles.reshape(16, 8, X).astype(BF16)
            else:
                tiles = tiles + dot(back, (rows - high.astype(F32)).astype(BF16))
                fout[:, 2 * w + i] = tiles.reshape(16, 8, X)


def kernel_d(scal, got, halo_l, halo_r, p3, mine, theirs, feat):
    core = scal[4]
    order = shuffle(False)
    for w in range(-1, Z + 1):
        for i in range(2):
            ref, t = (halo_l, 2 + i) if w < 0 else (halo_r, 2 + i) if w == Z else (got, w * TILES + 6 + i)
            rows = dot(order, tile(ref, t).astype(BF16))
            if w < 0:
                rows = jnp.where(scal[5] > 0, rows, 0.0)
            elif w == Z:
                rows = jnp.where(scal[6] > 0, rows, 0.0)
            for r in range(2):
                cols = slice((2 * i + r) * X, (2 * i + r + 1) * X)
                feat[(w + 1) * CIN : (w + 2) * CIN, cols] = rows[r * CIN : (r + 1) * CIN].astype(BF16)
    last = []
    for kh in range(3):
        total = None
        for s in range(Z):
            part = dot_t(p3[s], feat[s * CIN : (s + 3) * CIN, kh * X : (kh + 2) * X])
            total = part if total is None else total + part
        for kw in range(3):
            store_halves(core, mine, theirs, 3 * kh + kw, 7, 7, total[kw * 128 : (kw + 1) * 128, : 2 * CIN])
            last.append(total[kw * 128 : (kw + 1) * 128, 2 * CIN :])
    last.append(jnp.zeros((128, CIN), F32))
    for b in range(5):
        store_halves(core, mine, theirs, 9 + b, 7, 7, jnp.concatenate([last[b], last[b + 5]], axis=1))


VMEM, SMEM = pl.BlockSpec(memory_space=pltpu.VMEM), pl.BlockSpec(memory_space=pltpu.SMEM)


def call(body, args, outs, scratch, flops, scalars):
    return pl.pallas_call(
        body,
        out_shape=tuple(jax.ShapeDtypeStruct(shape, kind) for shape, kind in outs),
        in_specs=[SMEM] * scalars + [VMEM] * (len(args) - scalars),
        out_specs=(VMEM,) * len(outs),
        scratch_shapes=[pltpu.VMEM(shape, kind) for shape, kind in scratch],
        compiler_params=pltpu.CompilerParams(vmem_limit_bytes=24 * 1024 * 1024),
        cost_estimate=pl.CostEstimate(flops=flops, bytes_accessed=4 * 1024 * 1024, transcendentals=0),
    )(*args)


def pairs(rows, count, width):
    return jnp.stack([rows[:, i : i + 16] for i in range(count)], axis=2).swapaxes(0, 1).reshape(16, Z, width, 8, X)


def shards(features, pre_act, out_grad, weight_one, weight_two, dropout_seed, layer_offset):
    chan_pos, slab_pos, core = lax.axis_index(CHAN), lax.axis_index(SLAB), lax.axis_index("core")
    edge = ((0, 0), (1, 1), (0, 0), (0, 0))

    grad = jnp.pad(out_grad.transpose(1, 2, 0, 3), edge).reshape(Z, 17, 2, 8, X)
    pre = pre_act.transpose(1, 2, 0, 3).reshape(Z, 16, 2, 8, X)
    feat = jnp.pad(features.transpose(1, 2, 0, 3), edge).reshape(Z, 17, 1, 8, X)
    sent = jnp.concatenate([pairs(grad, 2, 4), pairs(pre, 1, 2), pairs(feat, 2, 2)], axis=2)
    got = lax.all_to_all(sent.reshape(16, Z * TILES, 8, X), CHAN, 0, 0, tiled=True)

    up = [(i, (i + 1) % 16) for i in range(16)]
    down = [((i + 1) % 16, i) for i in range(16)]
    has_l, has_r = slab_pos > 0, slab_pos < 15
    swap = [(0, 1), (1, 0)]
    halo_l = lax.ppermute(got[:, 3 * TILES + 4 :], SLAB, up)
    halo_r = lax.ppermute(got[:, 4:TILES], SLAB, down)
    scal = jnp.stack(
        [slab_pos * Z, chan_pos * R, layer_offset[0], dropout_seed[0], core, has_l.astype(jnp.int32), has_r.astype(jnp.int32)]
    )

    g3, hid, left, right = call(
        kernel_a,
        (got, weight_two),
        [((Z, 384, 4 * X), BF16), ((Z, MID, R * X), F32), ((MID, R * X), F32), ((MID, R * X), F32)],
        [((3, 384, 384), BF16)],
        10**9,
        0,
    )
    from_l = lax.ppermute(right, SLAB, up)
    from_r = lax.ppermute(left, SLAB, down)
    mask, mine_two, theirs_two = call(
        kernel_b,
        (scal, got, halo_l, halo_r, g3),
        [((Z, MID, R * X), BF16), ((14, 128, 128), F32), ((14, 128, 128), BF16)],
        [(((Z + 2) * MID, R * X), BF16)],
        4 * 10**9,
        1,
    )
    p3, feature, feature_l, feature_r = call(
        kernel_c,
        (scal, hid, from_l, from_r, mask, weight_one),
        [((Z, 384, R * X), BF16), ((16, 8, 8, X), F32), ((16, 2, 8, X), BF16), ((16, 2, 8, X), BF16)],
        [((9 * CIN, 384), BF16), ((Z + 2, CIN, 4 * X), F32)],
        2 * 10**9,
        1,
    )
    mine_one, theirs_one = call(
        kernel_d,
        (scal, got, halo_l, halo_r, p3),
        [((7, 128, 128), F32), ((7, 128, 128), BF16)],
        [(((Z + 2) * CIN, 4 * X), BF16)],
        2 * 10**9,
        1,
    )

    mine_two = mine_two + lax.ppermute(theirs_two, "core", swap).astype(F32)
    mine_one = mine_one + lax.ppermute(theirs_one, "core", swap).astype(F32)
    mine = jnp.concatenate([mine_two, mine_one]).astype(BF16).reshape(21, 16, 8, 128).transpose(1, 0, 2, 3)
    feature_l, feature_r = (
        jnp.where(has_l, lax.ppermute(feature_r, SLAB, up).astype(F32), 0.0),
        jnp.where(has_r, lax.ppermute(feature_l, SLAB, down).astype(F32), 0.0),
    )
    feature = jnp.concatenate(
        [feature[:, 0:2] + feature_l, feature[:, 2:6], feature[:, 6:8] + feature_r], axis=1
    ).astype(BF16)
    got = lax.all_to_all(jnp.concatenate([mine, feature], axis=1), CHAN, 0, 0, tiled=True)

    rows = got[:, 21:].astype(F32).reshape(16, Z, 4, 4, X)
    none = jnp.zeros((1, Z, 4, X), F32)
    first = rows[:, :, 1] + jnp.concatenate([none, rows[:-1, :, 3]])
    second = rows[:, :, 2] + jnp.concatenate([rows[1:, :, 0], none])
    feature = jnp.stack([first, second], axis=2).transpose(3, 1, 0, 2, 4).reshape(4, Z, NY, X)

    part = got[:, :21].astype(F32).sum(axis=0)
    part = part + lax.ppermute(part, "zl", swap)
    part = part + lax.ppermute(part, "x", [(i, i ^ 1) for i in range(4)])
    part = part + lax.ppermute(part, "x", [(i, i ^ 2) for i in range(4)])
    scale = 1.0 / math.sqrt(NZ * NY * X)
    total = lax.all_gather(part * scale, "core", axis=0, tiled=False)
    two = jnp.concatenate([total[0, :14], total[1, 1:14]])
    one = total[:, 14:].reshape(14, 8, 2, CIN)
    one = jnp.concatenate([one[:9, :, 0], one[:9, :, 1], one[9:, :, 0], one[9:13, :, 1]])
    two = two.transpose(1, 2, 0).reshape(8, 27 * MID)
    one = one.transpose(1, 2, 0).reshape(4, 54 * CIN)
    return feature, one, two


def solution(mesh):
    split = Mesh(mesh.devices.reshape(4, 2, 2, 4, 4), ("x", "zl", "core", "y", "zh"))
    cells = P(CHAN, SLAB, None, None)
    return jax.shard_map(
        shards,
        mesh=split,
        in_specs=(cells, cells, cells, P(), P(), P(), P()),
        out_specs=(cells, P(CHAN, None), P(CHAN, None)),
        check_vma=False,
    )
```

```python
import math

import jax
import jax.numpy as jnp
from jax import lax
from jax.experimental import pallas as pl
from jax.experimental.pallas import tpu as pltpu
from jax.sharding import Mesh
from jax.sharding import PartitionSpec as P

BF16, F32 = jnp.bfloat16, jnp.float32
CHAN, SLAB = ("y", "zh"), ("x", "zl", "core")
Z, R, X = 4, 2, 128
NZ, NY = 64, 32
MID, CIN = 128, 64
PRE, GRAD, FEAT = (0, 20, 22, 18), 2, 24


def kept_scale(offset, seed, z, h):
    c = lax.broadcasted_iota(jnp.int32, (MID, X), 0)
    w = lax.broadcasted_iota(jnp.int32, (MID, X), 1)
    position = ((c * NZ + z) * NY + h) * X + w
    m = (position + offset) ^ seed
    m = m * jnp.int32(739982445)
    m = m ^ lax.shift_right_logical(m, jnp.int32(15))
    m = m * jnp.int32(695938361)
    m = m ^ lax.shift_right_logical(m, jnp.int32(12))
    return jnp.where((m & 65535) < 52429, F32(1.25), F32(0.0))


def store_shifts(dst, plane, row, block):
    lane = lax.broadcasted_iota(jnp.int32, block.shape, 1)
    cols = slice(row * X, (row + 1) * X)
    ahead = jnp.where(lane == X - 1, 0.0, pltpu.roll(block, X - 1, 1))
    behind = jnp.where(lane == 0, 0.0, pltpu.roll(block, 1, 1))
    dst[plane, 0:128, cols] = ahead.astype(BF16)
    dst[plane, 128:256, cols] = block.astype(BF16)
    dst[plane, 256:384, cols] = behind.astype(BF16)


def dot(a, b):
    return lax.dot_general(a, b, (((1,), (0,)), ((), ())), preferred_element_type=F32)


def dot_t(a, b):
    return lax.dot_general(a, b, (((1,), (1,)), ((), ())), preferred_element_type=F32)


def tile(ref, t):
    return ref[:, t].astype(F32).reshape(128, X)


def store_halves(core, mine, theirs, s, count, step, slab):
    for me in range(2):

        @pl.when(core == me)
        def _():
            for half in range(2):
                if 0 <= s - half * step < count:
                    dst = mine if half == me else theirs
                    dst[s - half * step] = slab.astype(dst.dtype)


def shuffle(back):
    i = lax.broadcasted_iota(jnp.int32, (128, 128), 1 if back else 0)
    j = lax.broadcasted_iota(jnp.int32, (128, 128), 0 if back else 1)
    at = (lax.rem(i, 64) // 4) * 8 + (i // 64) * 4 + lax.rem(i, 4)
    return jnp.where(at == j, F32(1.0), F32(0.0)).astype(BF16)


def scaled(scal, pre, w, r):
    scale = kept_scale(scal[2], scal[3], scal[0] + w, scal[1] + r)
    return (jnp.maximum(pre, 0.0) * scale).astype(BF16), jnp.where(pre > 0, scale, 0.0)


def kernel_s(grad_in, pre_in, feat_in, sent, grad, pre, feat, rows8, rows4, sems):
    copies = [
        pltpu.make_async_copy(src, dst, sems.at[i])
        for i, (src, dst) in enumerate(((grad_in, grad), (pre_in, pre), (feat_in, feat)))
    ]
    for copy in copies:
        copy.start()
    sent[0, GRAD : GRAD + 4 * Z] = jnp.zeros((4 * Z, 8, X), BF16)
    sent[15, GRAD : GRAD + 4 * Z] = jnp.zeros((4 * Z, 8, X), BF16)
    rows4[...] = jnp.zeros_like(rows4)
    copies[0].wait()
    for z in range(Z):
        for c in range(8):
            rows8[z, pl.ds(c, NY, stride=8), :] = grad[c, z].astype(F32)
        rows = rows8[z].reshape(16, 2, 8, X).astype(BF16)
        at = GRAD + 4 * z
        sent[1:, at] = rows[:-1, 1]
        sent[:, at + 1] = rows[:, 0]
        sent[:, at + 2] = rows[:, 1]
        sent[:-1, at + 3] = rows[1:, 0]
    copies[1].wait()
    copies[2].wait()
    for z in range(Z):
        for c in range(8):
            rows8[Z + z, pl.ds(c, NY, stride=8), :] = pre[c, z].astype(F32)
        rows = rows8[Z + z].reshape(16, 2, 8, X).astype(BF16)
        sent[:, PRE[z]] = rows[:, 0]
        sent[:, PRE[z] + 1] = rows[:, 1]
        for c in range(4):
            rows4[z, pl.ds(4 + c, NY, stride=4), :] = feat[c, z].astype(F32)
        rows = rows4[z].reshape(17, 8, X).astype(BF16)
        sent[:, FEAT + 2 * z] = rows[:-1]
        sent[:, FEAT + 2 * z + 1] = rows[1:]


def add_feature_terms(fin, wf, rows, plane):
    first, end = max(0, 1 - plane), min(3, Z + 1 - plane)
    terms = dot(wf[first * 3 * CIN : end * 3 * CIN], rows)
    for kd in range(first, end):
        for kh in range(3):
            at = ((kd - first) * 3 + kh) * CIN
            cols = slice(kh * X, (kh + 2) * X)
            fin[plane - 1 + kd, :, cols] = fin[plane - 1 + kd, :, cols] + terms[at : at + CIN]


def raw_one_terms(feat, planes, total, kh):
    for plane, rows in planes:
        part = dot_t(rows, feat[(plane + 1) * CIN : (plane + 4) * CIN, kh * X : (kh + 2) * X])
        total = part if total is None else total + part
    return total


def kernel_a(scal, got, w_two, w_one, g3, hid, mask, two, wk, feat, wf, fin, one, act, p3):
    for kd in range(3):
        for kh in range(3):
            for kw in range(3):
                wk[kh, kd * MID : (kd + 1) * MID, kw * 128 : (kw + 1) * 128] = w_two[9 * kd + 3 * kh + kw]
    for z in range(Z):
        for r in range(4):
            store_shifts(g3, z, r, tile(got, GRAD + 4 * z + r))
    hid[...] = jnp.zeros_like(hid)
    for z in range(Z):
        total = None
        for kh in range(3):
            part = dot(wk[kh], g3[z, :, (2 - kh) * X : (4 - kh) * X])
            total = part if total is None else total + part
        for kd in range(3):
            hid[z + kd] = hid[z + kd] + total[kd * MID : (kd + 1) * MID]
    act[...] = jnp.zeros_like(act)
    for w in range(Z):
        for r in range(R):
            cols = slice(r * X, (r + 1) * X)
            hidden, kept = scaled(scal, tile(got, PRE[w] + r), w, r)
            act[(w + 1) * MID : (w + 2) * MID, cols] = hidden
            mask[w, :, cols] = kept.astype(BF16)
    for kh in range(3):
        total = None
        for s in range(Z):
            part = dot_t(g3[s, :, (2 - kh) * X : (4 - kh) * X], act[s * MID : (s + 3) * MID])
            total = part if total is None else total + part
        two[kh] = total
    order = shuffle(False)
    feat[...] = jnp.zeros_like(feat)
    for w in range(Z):
        for i in range(2):
            rows = dot(order, tile(got, FEAT + 2 * w + i).astype(BF16)).astype(BF16)
            for r in range(2):
                cols = slice((2 * i + r) * X, (2 * i + r + 1) * X)
                feat[(w + 2) * CIN : (w + 3) * CIN, cols] = rows[r * CIN : (r + 1) * CIN]
    for kd in range(3):
        for kh in range(3):
            for kw in range(3):
                at = (kd * 3 + kh) * CIN
                wf[at : at + CIN, kw * 128 : (kw + 1) * 128] = w_one[9 * kd + 3 * kh + kw]
    fin[...] = jnp.zeros_like(fin)
    for at, z in enumerate((1, 2)):
        for r in range(R):
            cols = slice(r * X, (r + 1) * X)
            store_shifts(p3, at, r, hid[z + 1, :, cols] * mask[z, :, cols].astype(F32))
        add_feature_terms(fin, wf, p3[at], z)
    for kh in range(3):
        one[kh] = raw_one_terms(feat, ((1, p3[0]), (2, p3[1])), None, kh)


def kernel_c(
    scal, halo_l, halo_r, g3, part_hid, mask, part_two, wk, feat, wf, part_fin, part_one,
    fout, mine, theirs, mine_one, theirs_one, g, hid, act, p3, fin,
):
    core, has_l, has_r = scal[4], scal[5] > 0, scal[6] > 0
    for at in range(4):
        for r in range(4):
            if at < 2:
                store_shifts(g, at, r, jnp.where(has_l, tile(halo_l, 4 * at + r), 0.0))
            else:
                store_shifts(g, at, r, jnp.where(has_r, tile(halo_r, 4 * at - 6 + r), 0.0))
    hid[...] = part_hid[...]
    for at, plane, first, end in ((0, -2, 2, 3), (1, -1, 1, 3), (2, 4, 0, 2), (3, 5, 0, 1)):
        total = None
        for kh in range(3):
            part = dot(wk[kh, first * MID : end * MID], g[at, :, (2 - kh) * X : (4 - kh) * X])
            total = part if total is None else total + part
        for kd in range(first, end):
            hid[plane + kd] = hid[plane + kd] + total[(kd - first) * MID : (kd - first + 1) * MID]
    outer = (-1, 0, Z - 1, Z)
    for at, plane in enumerate(outer):
        j = plane + 1
        for r in range(R):
            cols = slice(r * X, (r + 1) * X)
            if j == 0:
                hidden, kept = scaled(scal, jnp.where(has_l, tile(halo_l, 8 + r), 0.0), -1, r)
                act[0, :, cols] = hidden
            elif j == Z + 1:
                hidden, kept = scaled(scal, jnp.where(has_r, tile(halo_r, r), 0.0), Z, r)
                act[1, :, cols] = hidden
            else:
                kept = mask[j - 1, :, cols].astype(F32)
            store_shifts(p3, at, r, hid[j, :, cols] * kept)
    for kh in range(3):
        rows = slice((2 - kh) * X, (4 - kh) * X)
        low = dot_t(g3[0, :, rows], act[0])
        high = dot_t(g3[Z - 1, :, rows], act[1])
        for kd in range(3):
            for kw in range(3):
                slab = part_two[kh, kw * 128 : (kw + 1) * 128, kd * MID : (kd + 1) * MID]
                if kd != 1:
                    slab = slab + (low if kd == 0 else high)[kw * 128 : (kw + 1) * 128]
                store_halves(core, mine, theirs, 9 * kd + 3 * kh + kw, 14, 13, slab)
    fin[...] = part_fin[...]
    for at, plane in enumerate(outer):
        add_feature_terms(fin, wf, p3[at], plane)
    back = shuffle(True)
    for w in range(Z):
        for i in range(2):
            rows = jnp.concatenate([fin[w, :, (2 * i + r) * X : (2 * i + r + 1) * X] for r in range(2)], axis=0)
            fout[:, 2 * w + i] = dot(back, rows.astype(BF16)).reshape(16, 8, X).astype(BF16)
    last = []
    for kh in range(3):
        total = raw_one_terms(feat, [(plane, p3[at]) for at, plane in enumerate(outer)], part_one[kh], kh)
        for kw in range(3):
            store_halves(core, mine_one, theirs_one, 3 * kh + kw, 7, 7, total[kw * 128 : (kw + 1) * 128, : 2 * CIN])
            last.append(total[kw * 128 : (kw + 1) * 128, 2 * CIN :])
    last.append(jnp.zeros((128, CIN), F32))
    for b in range(5):
        store_halves(core, mine_one, theirs_one, 9 + b, 7, 7, jnp.concatenate([last[b], last[b + 5]], axis=1))


VMEM, SMEM = pl.BlockSpec(memory_space=pltpu.VMEM), pl.BlockSpec(memory_space=pltpu.SMEM)


def call(body, args, outs, scratch, flops, scalars):
    return pl.pallas_call(
        body,
        out_shape=tuple(jax.ShapeDtypeStruct(shape, kind) for shape, kind in outs),
        in_specs=[SMEM] * scalars + [VMEM] * (len(args) - scalars),
        out_specs=(VMEM,) * len(outs),
        scratch_shapes=[pltpu.VMEM(shape, kind) for shape, kind in scratch],
        compiler_params=pltpu.CompilerParams(vmem_limit_bytes=24 * 1024 * 1024),
        cost_estimate=pl.CostEstimate(flops=flops, bytes_accessed=4 * 1024 * 1024, transcendentals=0),
    )(*args)


def shards(features, pre_act, out_grad, weight_one, weight_two, dropout_seed, layer_offset):
    chan_pos, slab_pos, core = lax.axis_index(CHAN), lax.axis_index(SLAB), lax.axis_index("core")

    anywhere = pl.BlockSpec(memory_space=pl.ANY)
    sent = pl.pallas_call(
        kernel_s,
        out_shape=jax.ShapeDtypeStruct((16, 32, 8, X), BF16),
        in_specs=[anywhere] * 3,
        out_specs=VMEM,
        scratch_shapes=[
            pltpu.VMEM(out_grad.shape, BF16),
            pltpu.VMEM(pre_act.shape, BF16),
            pltpu.VMEM(features.shape, BF16),
            pltpu.VMEM((2 * Z, NY * 8, X), F32),
            pltpu.VMEM((Z, (NY + 2) * 4, X), F32),
            pltpu.SemaphoreType.DMA((3,)),
        ],
        compiler_params=pltpu.CompilerParams(vmem_limit_bytes=56 * 1024 * 1024),
    )(out_grad, pre_act, features)
    got = lax.all_to_all(sent, CHAN, 0, 0, tiled=True)

    up = [(i, (i + 1) % 16) for i in range(16)]
    down = [((i + 1) % 16, i) for i in range(16)]
    swap = [(0, 1), (1, 0)]
    halo_l = lax.ppermute(got[:, 10:20], SLAB, up)
    halo_r = lax.ppermute(got[:, :10], SLAB, down)
    has_l, has_r = slab_pos > 0, slab_pos < 15
    scal = jnp.stack(
        [slab_pos * Z, chan_pos * R, layer_offset[0], dropout_seed[0], core, has_l.astype(jnp.int32), has_r.astype(jnp.int32)]
    )

    own = call(
        kernel_a,
        (scal, got, weight_two, weight_one),
        [
            ((Z, 384, 4 * X), BF16),
            ((Z + 2, MID, R * X), F32),
            ((Z, MID, R * X), BF16),
            ((3, 384, 384), F32),
            ((3, 384, 384), BF16),
            (((Z + 4) * CIN, 4 * X), BF16),
            ((9 * CIN, 384), BF16),
            ((Z, CIN, 4 * X), F32),
            ((3, 384, 3 * CIN), F32),
        ],
        [(((Z + 2) * MID, R * X), BF16), ((2, 384, R * X), BF16)],
        6 * 10**9,
        1,
    )
    feature, mine_two, theirs_two, mine_one, theirs_one = call(
        kernel_c,
        (scal, halo_l, halo_r) + tuple(own),
        [
            ((16, 8, 8, X), BF16),
            ((14, 128, 128), F32),
            ((14, 128, 128), BF16),
            ((7, 128, 128), F32),
            ((7, 128, 128), BF16),
        ],
        [
            ((4, 384, 4 * X), BF16),
            ((Z + 2, MID, R * X), F32),
            ((2, MID, R * X), BF16),
            ((4, 384, R * X), BF16),
            ((Z, CIN, 4 * X), F32),
        ],
        3 * 10**9,
        1,
    )

    mine_two = mine_two + lax.ppermute(theirs_two, "core", swap).astype(F32)
    mine_one = mine_one + lax.ppermute(theirs_one, "core", swap).astype(F32)
    mine = jnp.concatenate([mine_two, mine_one]).astype(BF16).reshape(21, 16, 8, 128).transpose(1, 0, 2, 3)
    got = lax.all_to_all(jnp.concatenate([mine, feature], axis=1), CHAN, 0, 0, tiled=True)

    rows = got[:, 21:].astype(F32).reshape(16, Z, 4, 4, X)
    none = jnp.zeros((1, Z, 4, X), F32)
    first = rows[:, :, 1] + jnp.concatenate([none, rows[:-1, :, 3]])
    second = rows[:, :, 2] + jnp.concatenate([rows[1:, :, 0], none])
    feature = jnp.stack([first, second], axis=2).transpose(3, 1, 0, 2, 4).reshape(4, Z, NY, X)

    part = got[:, :21].astype(F32).sum(axis=0)
    part = part + lax.ppermute(part, "zl", swap)
    part = part + lax.ppermute(part, "x", [(i, i ^ 1) for i in range(4)])
    part = part + lax.ppermute(part, "x", [(i, i ^ 2) for i in range(4)])
    scale = 1.0 / math.sqrt(NZ * NY * X)
    total = lax.all_gather(part * scale, "core", axis=0, tiled=False)
    two = jnp.concatenate([total[0, :14], total[1, 1:14]])
    one = total[:, 14:].reshape(14, 8, 2, CIN)
    one = jnp.concatenate([one[:9, :, 0], one[:9, :, 1], one[9:, :, 0], one[9:13, :, 1]])
    two = two.transpose(1, 2, 0).reshape(8, 27 * MID)
    one = one.transpose(1, 2, 0).reshape(4, 54 * CIN)
    return feature, one, two


def solution(mesh):
    split = Mesh(mesh.devices.reshape(4, 2, 2, 4, 4), ("x", "zl", "core", "y", "zh"))
    cells = P(CHAN, SLAB, None, None)
    return jax.shard_map(
        shards,
        mesh=split,
        in_specs=(cells, cells, cells, P(), P(), P(), P()),
        out_specs=(cells, P(CHAN, None), P(CHAN, None)),
        check_vma=False,
    )
```

```python
import math

import jax
import jax.numpy as jnp
from jax import lax
from jax.experimental import pallas as pl
from jax.experimental.pallas import tpu as pltpu
from jax.sharding import Mesh
from jax.sharding import PartitionSpec as P

BF16, F32 = jnp.bfloat16, jnp.float32
CHAN, SLAB = ("y", "zh"), ("x", "zl", "core")
Z, R, X = 4, 2, 128
NZ, NY = 64, 32
MID, CIN = 128, 64
PRE, GRAD, FEAT = (0, 20, 22, 18), 2, 24


def kept_scale(offset, seed, z, h):
    c = lax.broadcasted_iota(jnp.int32, (MID, X), 0)
    w = lax.broadcasted_iota(jnp.int32, (MID, X), 1)
    position = ((c * NZ + z) * NY + h) * X + w
    m = (position + offset) ^ seed
    m = m * jnp.int32(739982445)
    m = m ^ lax.shift_right_logical(m, jnp.int32(15))
    m = m * jnp.int32(695938361)
    m = m ^ lax.shift_right_logical(m, jnp.int32(12))
    return jnp.where((m & 65535) < 52429, F32(1.25), F32(0.0))


def store_shifts(dst, plane, row, block):
    lane = lax.broadcasted_iota(jnp.int32, block.shape, 1)
    cols = slice(row * X, (row + 1) * X)
    ahead = jnp.where(lane == X - 1, 0.0, pltpu.roll(block, X - 1, 1))
    behind = jnp.where(lane == 0, 0.0, pltpu.roll(block, 1, 1))
    dst[plane, 0:128, cols] = ahead.astype(BF16)
    dst[plane, 128:256, cols] = block.astype(BF16)
    dst[plane, 256:384, cols] = behind.astype(BF16)


def dot(a, b):
    return lax.dot_general(a, b, (((1,), (0,)), ((), ())), preferred_element_type=F32)


def dot_t(a, b):
    return lax.dot_general(a, b, (((1,), (1,)), ((), ())), preferred_element_type=F32)


def tile(ref, t):
    return ref[:, t].astype(F32).reshape(128, X)


def store_slab(core, mine, theirs, s, slab):
    at = s // 6 * 3 + s % 3
    owner = s // 3 % 2

    @pl.when(core == owner)
    def _():
        mine[at] = slab

    @pl.when(core != owner)
    def _():
        theirs[at] = slab.astype(BF16)


def shuffle(back):
    i = lax.broadcasted_iota(jnp.int32, (128, 128), 1 if back else 0)
    j = lax.broadcasted_iota(jnp.int32, (128, 128), 0 if back else 1)
    at = (lax.rem(i, 64) // 4) * 8 + (i // 64) * 4 + lax.rem(i, 4)
    return jnp.where(at == j, F32(1.0), F32(0.0)).astype(BF16)


def scaled(scal, pre, w, r):
    scale = kept_scale(scal[2], scal[3], scal[0] + w, scal[1] + r)
    return (jnp.maximum(pre, 0.0) * scale).astype(BF16), jnp.where(pre > 0, scale, 0.0)


def kernel_s(grad_in, pre_in, feat_in, sent, grad, pre, feat, rows8, rows4, sems):
    copies = [
        pltpu.make_async_copy(src, dst, sems.at[i])
        for i, (src, dst) in enumerate(((grad_in, grad), (pre_in, pre), (feat_in, feat)))
    ]
    for copy in copies:
        copy.start()
    sent[0, GRAD : GRAD + 4 * Z] = jnp.zeros((4 * Z, 8, X), BF16)
    sent[15, GRAD : GRAD + 4 * Z] = jnp.zeros((4 * Z, 8, X), BF16)
    rows4[...] = jnp.zeros_like(rows4)
    copies[0].wait()
    for z in range(Z):
        for c in range(8):
            rows8[z, pl.ds(c, NY, stride=8), :] = grad[c, z].astype(F32)
        rows = rows8[z].reshape(16, 2, 8, X).astype(BF16)
        at = GRAD + 4 * z
        sent[1:, at] = rows[:-1, 1]
        sent[:, at + 1] = rows[:, 0]
        sent[:, at + 2] = rows[:, 1]
        sent[:-1, at + 3] = rows[1:, 0]
    copies[1].wait()
    copies[2].wait()
    for z in range(Z):
        for c in range(8):
            rows8[Z + z, pl.ds(c, NY, stride=8), :] = pre[c, z].astype(F32)
        rows = rows8[Z + z].reshape(16, 2, 8, X).astype(BF16)
        sent[:, PRE[z]] = rows[:, 0]
        sent[:, PRE[z] + 1] = rows[:, 1]
        for c in range(4):
            rows4[z, pl.ds(4 + c, NY, stride=4), :] = feat[c, z].astype(F32)
        rows = rows4[z].reshape(17, 8, X).astype(BF16)
        sent[:, FEAT + 2 * z] = rows[:-1]
        sent[:, FEAT + 2 * z + 1] = rows[1:]


def add_feature_terms(fin, wf, rows, plane):
    first, end = max(0, 1 - plane), min(3, Z + 1 - plane)
    terms = dot(wf[first * 3 * CIN : end * 3 * CIN], rows)
    for kd in range(first, end):
        for kh in range(3):
            at = ((kd - first) * 3 + kh) * CIN
            cols = slice(kh * X, (kh + 2) * X)
            fin[plane - 1 + kd, :, cols] = fin[plane - 1 + kd, :, cols] + terms[at : at + CIN]


def raw_one_terms(feat, planes, total, kh):
    for plane, rows in planes:
        part = dot_t(rows, feat[(plane + 1) * CIN : (plane + 4) * CIN, kh * X : (kh + 2) * X])
        total = part if total is None else total + part
    return total


def kernel_a(scal, got, w_two, w_one, g3, hid, mask, two, wk, feat, wf, fin, one, act, p3):
    for kd in range(3):
        for kh in range(3):
            for kw in range(3):
                wk[kh, kd * MID : (kd + 1) * MID, kw * 128 : (kw + 1) * 128] = w_two[9 * kd + 3 * kh + kw]
    for z in range(Z):
        for r in range(4):
            store_shifts(g3, z, r, tile(got, GRAD + 4 * z + r))
    hid[...] = jnp.zeros_like(hid)
    for z in range(Z):
        total = None
        for kh in range(3):
            part = dot(wk[kh], g3[z, :, (2 - kh) * X : (4 - kh) * X])
            total = part if total is None else total + part
        for kd in range(3):
            hid[z + kd] = hid[z + kd] + total[kd * MID : (kd + 1) * MID]
    act[...] = jnp.zeros_like(act)
    for w in range(Z):
        for r in range(R):
            cols = slice(r * X, (r + 1) * X)
            hidden, kept = scaled(scal, tile(got, PRE[w] + r), w, r)
            act[(w + 1) * MID : (w + 2) * MID, cols] = hidden
            mask[w, :, cols] = kept.astype(BF16)
    for kh in range(3):
        total = None
        for s in range(Z):
            part = dot_t(g3[s, :, (2 - kh) * X : (4 - kh) * X], act[s * MID : (s + 3) * MID])
            total = part if total is None else total + part
        two[kh] = total
    order = shuffle(False)
    feat[...] = jnp.zeros_like(feat)
    for w in range(Z):
        for i in range(2):
            rows = dot(order, tile(got, FEAT + 2 * w + i).astype(BF16)).astype(BF16)
            for r in range(2):
                cols = slice((2 * i + r) * X, (2 * i + r + 1) * X)
                feat[(w + 2) * CIN : (w + 3) * CIN, cols] = rows[r * CIN : (r + 1) * CIN]
    for kd in range(3):
        for kh in range(3):
            for kw in range(3):
                at = (kd * 3 + kh) * CIN
                wf[at : at + CIN, kw * 128 : (kw + 1) * 128] = w_one[9 * kd + 3 * kh + kw]
    fin[...] = jnp.zeros_like(fin)
    for at, z in enumerate((1, 2)):
        for r in range(R):
            cols = slice(r * X, (r + 1) * X)
            store_shifts(p3, at, r, hid[z + 1, :, cols] * mask[z, :, cols].astype(F32))
        add_feature_terms(fin, wf, p3[at], z)
    for kh in range(3):
        one[kh] = raw_one_terms(feat, ((1, p3[0]), (2, p3[1])), None, kh)


def kernel_c(
    scal, halo_l, halo_r, g3, part_hid, mask, part_two, wk, feat, wf, part_fin, part_one,
    fout, mine, theirs, g, hid, act, p3, fin,
):
    core, has_l, has_r = scal[4], scal[5] > 0, scal[6] > 0
    mine[20:] = jnp.zeros((4, 128, 128), F32)
    theirs[20:] = jnp.zeros((4, 128, 128), BF16)
    for at in range(4):
        for r in range(4):
            if at < 2:
                store_shifts(g, at, r, jnp.where(has_l, tile(halo_l, 4 * at + r), 0.0))
            else:
                store_shifts(g, at, r, jnp.where(has_r, tile(halo_r, 4 * at - 6 + r), 0.0))
    hid[...] = part_hid[...]
    for at, plane, first, end in ((0, -2, 2, 3), (1, -1, 1, 3), (2, 4, 0, 2), (3, 5, 0, 1)):
        total = None
        for kh in range(3):
            part = dot(wk[kh, first * MID : end * MID], g[at, :, (2 - kh) * X : (4 - kh) * X])
            total = part if total is None else total + part
        for kd in range(first, end):
            hid[plane + kd] = hid[plane + kd] + total[(kd - first) * MID : (kd - first + 1) * MID]
    outer = (-1, 0, Z - 1, Z)
    for at, plane in enumerate(outer):
        j = plane + 1
        for r in range(R):
            cols = slice(r * X, (r + 1) * X)
            if j == 0:
                hidden, kept = scaled(scal, jnp.where(has_l, tile(halo_l, 8 + r), 0.0), -1, r)
                act[0, :, cols] = hidden
            elif j == Z + 1:
                hidden, kept = scaled(scal, jnp.where(has_r, tile(halo_r, r), 0.0), Z, r)
                act[1, :, cols] = hidden
            else:
                kept = mask[j - 1, :, cols].astype(F32)
            store_shifts(p3, at, r, hid[j, :, cols] * kept)
    for kh in range(3):
        rows = slice((2 - kh) * X, (4 - kh) * X)
        low = dot_t(g3[0, :, rows], act[0])
        high = dot_t(g3[Z - 1, :, rows], act[1])
        for kd in range(3):
            for kw in range(3):
                slab = part_two[kh, kw * 128 : (kw + 1) * 128, kd * MID : (kd + 1) * MID]
                if kd != 1:
                    slab = slab + (low if kd == 0 else high)[kw * 128 : (kw + 1) * 128]
                store_slab(core, mine, theirs, 9 * kd + 3 * kh + kw, slab)
    fin[...] = part_fin[...]
    for at, plane in enumerate(outer):
        add_feature_terms(fin, wf, p3[at], plane)
    back = shuffle(True)
    for w in range(Z):
        for i in range(2):
            rows = jnp.concatenate([fin[w, :, (2 * i + r) * X : (2 * i + r + 1) * X] for r in range(2)], axis=0)
            fout[:, 2 * w + i] = dot(back, rows.astype(BF16)).reshape(16, 8, X).astype(BF16)
    last = []
    for kh in range(3):
        total = raw_one_terms(feat, [(plane, p3[at]) for at, plane in enumerate(outer)], part_one[kh], kh)
        for kw in range(3):
            store_slab(core, mine, theirs, 27 + 3 * kh + kw, total[kw * 128 : (kw + 1) * 128, : 2 * CIN])
            last.append(total[kw * 128 : (kw + 1) * 128, 2 * CIN :])
    last.append(jnp.zeros((128, CIN), F32))
    for b in range(5):
        store_slab(core, mine, theirs, 36 + b, jnp.concatenate([last[b], last[b + 5]], axis=1))


def kernel_p(shares, feature, sent):
    for i in range(3):
        total = shares[0, i].astype(F32)
        for j in range(1, 8):
            total = total + shares[j, i].astype(F32)
        high = total.astype(BF16).astype(F32)
        sent[:, i] = high.reshape(16, 8, X).astype(BF16)
        sent[:, 3 + i] = (total - high).reshape(16, 8, X).astype(BF16)
    sent[:, 6:] = feature[...]


VMEM, SMEM = pl.BlockSpec(memory_space=pltpu.VMEM), pl.BlockSpec(memory_space=pltpu.SMEM)


def call(body, args, outs, scratch, flops, scalars):
    return pl.pallas_call(
        body,
        out_shape=tuple(jax.ShapeDtypeStruct(shape, kind) for shape, kind in outs),
        in_specs=[SMEM] * scalars + [VMEM] * (len(args) - scalars),
        out_specs=(VMEM,) * len(outs),
        scratch_shapes=[pltpu.VMEM(shape, kind) for shape, kind in scratch],
        compiler_params=pltpu.CompilerParams(vmem_limit_bytes=24 * 1024 * 1024),
        cost_estimate=pl.CostEstimate(flops=flops, bytes_accessed=4 * 1024 * 1024, transcendentals=0),
    )(*args)


def shards(features, pre_act, out_grad, weight_one, weight_two, dropout_seed, layer_offset):
    chan_pos, slab_pos, core = lax.axis_index(CHAN), lax.axis_index(SLAB), lax.axis_index("core")

    anywhere = pl.BlockSpec(memory_space=pl.ANY)
    sent = pl.pallas_call(
        kernel_s,
        out_shape=jax.ShapeDtypeStruct((16, 32, 8, X), BF16),
        in_specs=[anywhere] * 3,
        out_specs=VMEM,
        scratch_shapes=[
            pltpu.VMEM(out_grad.shape, BF16),
            pltpu.VMEM(pre_act.shape, BF16),
            pltpu.VMEM(features.shape, BF16),
            pltpu.VMEM((2 * Z, NY * 8, X), F32),
            pltpu.VMEM((Z, (NY + 2) * 4, X), F32),
            pltpu.SemaphoreType.DMA((3,)),
        ],
        compiler_params=pltpu.CompilerParams(vmem_limit_bytes=56 * 1024 * 1024),
    )(out_grad, pre_act, features)
    got = lax.all_to_all(sent, CHAN, 0, 0, tiled=True)

    up = [(i, (i + 1) % 16) for i in range(16)]
    down = [((i + 1) % 16, i) for i in range(16)]
    swap = [(0, 1), (1, 0)]
    halo_l = lax.ppermute(got[:, 10:20], SLAB, up)
    halo_r = lax.ppermute(got[:, :10], SLAB, down)
    has_l, has_r = slab_pos > 0, slab_pos < 15
    scal = jnp.stack(
        [slab_pos * Z, chan_pos * R, layer_offset[0], dropout_seed[0], core, has_l.astype(jnp.int32), has_r.astype(jnp.int32)]
    )

    own = call(
        kernel_a,
        (scal, got, weight_two, weight_one),
        [
            ((Z, 384, 4 * X), BF16),
            ((Z + 2, MID, R * X), F32),
            ((Z, MID, R * X), BF16),
            ((3, 384, 384), F32),
            ((3, 384, 384), BF16),
            (((Z + 4) * CIN, 4 * X), BF16),
            ((9 * CIN, 384), BF16),
            ((Z, CIN, 4 * X), F32),
            ((3, 384, 3 * CIN), F32),
        ],
        [(((Z + 2) * MID, R * X), BF16), ((2, 384, R * X), BF16)],
        6 * 10**9,
        1,
    )
    feature, mine, theirs = call(
        kernel_c,
        (scal, halo_l, halo_r) + tuple(own),
        [
            ((16, 8, 8, X), BF16),
            ((24, 128, 128), F32),
            ((24, 128, 128), BF16),
        ],
        [
            ((4, 384, 4 * X), BF16),
            ((Z + 2, MID, R * X), F32),
            ((2, MID, R * X), BF16),
            ((4, 384, R * X), BF16),
            ((Z, CIN, 4 * X), F32),
        ],
        3 * 10**9,
        1,
    )

    mine = (mine + lax.ppermute(theirs, "core", swap).astype(F32)).astype(BF16)
    shares = lax.all_to_all(mine.reshape(8, 3, 128, 128), ("x", "zl"), 0, 0, tiled=True)
    (sent,) = call(kernel_p, (shares, feature), [((16, 14, 8, X), BF16)], [], 10**6, 0)
    got = lax.all_to_all(sent, CHAN, 0, 0, tiled=True)

    rows = got[:, 6:].astype(F32).reshape(16, Z, 4, 4, X)
    none = jnp.zeros((1, Z, 4, X), F32)
    first = rows[:, :, 1] + jnp.concatenate([none, rows[:-1, :, 3]])
    second = rows[:, :, 2] + jnp.concatenate([rows[1:, :, 0], none])
    feature = jnp.stack([first, second], axis=2).transpose(3, 1, 0, 2, 4).reshape(4, Z, NY, X)

    scale = 1.0 / math.sqrt(NZ * NY * X)
    part = got[:, :6].astype(F32).sum(axis=0)
    part = (part[:3] + part[3:]) * scale
    total = lax.all_to_all(jnp.broadcast_to(part[None], (16, 3, 8, 128)), SLAB, 0, 0, tiled=True)
    total = total.reshape(48, 8, 128)
    two, one = total[:27], total[27:41].reshape(14, 8, 2, CIN)
    one = jnp.concatenate([one[:9, :, 0], one[:9, :, 1], one[9:, :, 0], one[9:13, :, 1]])
    two = two.transpose(1, 2, 0).reshape(8, 27 * MID)
    one = one.transpose(1, 2, 0).reshape(4, 54 * CIN)
    return feature, one, two


def solution(mesh):
    split = Mesh(mesh.devices.reshape(4, 2, 2, 4, 4), ("x", "zl", "core", "y", "zh"))
    cells = P(CHAN, SLAB, None, None)
    return jax.shard_map(
        shards,
        mesh=split,
        in_specs=(cells, cells, cells, P(), P(), P(), P()),
        out_specs=(cells, P(CHAN, None), P(CHAN, None)),
        check_vma=False,
    )
```

```python
import math

import jax
import jax.numpy as jnp
from jax import lax
from jax.experimental import pallas as pl
from jax.experimental.pallas import tpu as pltpu
from jax.sharding import Mesh
from jax.sharding import PartitionSpec as P

BF16, F32 = jnp.bfloat16, jnp.float32
CHAN, SLAB = ("y", "zh"), ("x", "zl", "core")
Z, R, X = 4, 2, 128
NZ, NY = 64, 32
MID, CIN = 128, 64
PRE, GRAD, FEAT = (0, 20, 22, 18), 2, 24


def kept_scale(offset, seed, z, h):
    c = lax.broadcasted_iota(jnp.int32, (MID, X), 0)
    w = lax.broadcasted_iota(jnp.int32, (MID, X), 1)
    position = ((c * NZ + z) * NY + h) * X + w
    m = (position + offset) ^ seed
    m = m * jnp.int32(739982445)
    m = m ^ lax.shift_right_logical(m, jnp.int32(15))
    m = m * jnp.int32(695938361)
    m = m ^ lax.shift_right_logical(m, jnp.int32(12))
    return jnp.where((m & 65535) < 52429, F32(1.25), F32(0.0))


def store_shifts(dst, plane, row, block):
    lane = lax.broadcasted_iota(jnp.int32, block.shape, 1)
    cols = slice(row * X, (row + 1) * X)
    ahead = jnp.where(lane == X - 1, 0.0, pltpu.roll(block, X - 1, 1))
    behind = jnp.where(lane == 0, 0.0, pltpu.roll(block, 1, 1))
    dst[plane, 0:128, cols] = ahead.astype(BF16)
    dst[plane, 128:256, cols] = block.astype(BF16)
    dst[plane, 256:384, cols] = behind.astype(BF16)


def dot(a, b):
    return lax.dot_general(a, b, (((1,), (0,)), ((), ())), preferred_element_type=F32)


def dot_t(a, b):
    return lax.dot_general(a, b, (((1,), (1,)), ((), ())), preferred_element_type=F32)


def tile(ref, t):
    return ref[:, t].astype(F32).reshape(128, X)


def store_slab(core, slabs, s, slab):
    slabs[core ^ (s // 3 % 2), s // 6 * 3 + s % 3] = slab


def shuffle(back):
    i = lax.broadcasted_iota(jnp.int32, (128, 128), 1 if back else 0)
    j = lax.broadcasted_iota(jnp.int32, (128, 128), 0 if back else 1)
    at = (lax.rem(i, 64) // 4) * 8 + (i // 64) * 4 + lax.rem(i, 4)
    return jnp.where(at == j, F32(1.0), F32(0.0)).astype(BF16)


def scaled(pre, scale):
    return (jnp.maximum(pre, 0.0) * scale).astype(BF16), jnp.where(pre > 0, scale, 0.0)


def kernel_s(grad_in, pre_in, feat_in, sent, grad, pre, feat, rows8, rows4, sems):
    copies = [
        pltpu.make_async_copy(src, dst, sems.at[i])
        for i, (src, dst) in enumerate(((grad_in, grad), (pre_in, pre), (feat_in, feat)))
    ]
    for copy in copies:
        copy.start()
    sent[0, GRAD : GRAD + 4 * Z] = jnp.zeros((4 * Z, 8, X), BF16)
    sent[15, GRAD : GRAD + 4 * Z] = jnp.zeros((4 * Z, 8, X), BF16)
    rows4[...] = jnp.zeros_like(rows4)
    copies[0].wait()
    for z in range(Z):
        for c in range(8):
            rows8[z, pl.ds(c, NY, stride=8), :] = grad[c, z].astype(F32)
        rows = rows8[z].reshape(16, 2, 8, X).astype(BF16)
        at = GRAD + 4 * z
        sent[1:, at] = rows[:-1, 1]
        sent[:, at + 1] = rows[:, 0]
        sent[:, at + 2] = rows[:, 1]
        sent[:-1, at + 3] = rows[1:, 0]
    copies[1].wait()
    copies[2].wait()
    for z in range(Z):
        for c in range(8):
            rows8[Z + z, pl.ds(c, NY, stride=8), :] = pre[c, z].astype(F32)
        rows = rows8[Z + z].reshape(16, 2, 8, X).astype(BF16)
        sent[:, PRE[z]] = rows[:, 0]
        sent[:, PRE[z] + 1] = rows[:, 1]
        for c in range(4):
            rows4[z, pl.ds(4 + c, NY, stride=4), :] = feat[c, z].astype(F32)
        rows = rows4[z].reshape(17, 8, X).astype(BF16)
        sent[:, FEAT + 2 * z] = rows[:-1]
        sent[:, FEAT + 2 * z + 1] = rows[1:]


def add_feature_terms(fin, wf, rows, plane):
    first, end = max(0, 1 - plane), min(3, Z + 1 - plane)
    terms = dot(wf[first * 3 * CIN : end * 3 * CIN], rows)
    for kd in range(first, end):
        for kh in range(3):
            at = ((kd - first) * 3 + kh) * CIN
            cols = slice(kh * X, (kh + 2) * X)
            fin[plane - 1 + kd, :, cols] = fin[plane - 1 + kd, :, cols] + terms[at : at + CIN]


def raw_one_terms(feat, planes, total, kh):
    for plane, rows in planes:
        part = dot_t(rows, feat[(plane + 1) * CIN : (plane + 4) * CIN, kh * X : (kh + 2) * X])
        total = part if total is None else total + part
    return total


def kernel_a(scal, got, w_two, w_one, g3, hid, mask, edge, two, wk, feat, wf, fin, one, act, p3):
    for kd in range(3):
        for kh in range(3):
            for kw in range(3):
                wk[kh, kd * MID : (kd + 1) * MID, kw * 128 : (kw + 1) * 128] = w_two[9 * kd + 3 * kh + kw]
    for z in range(Z):
        for r in range(4):
            store_shifts(g3, z, r, tile(got, GRAD + 4 * z + r))
    hid[...] = jnp.zeros_like(hid)
    for z in range(Z):
        total = None
        for kh in range(3):
            part = dot(wk[kh], g3[z, :, (2 - kh) * X : (4 - kh) * X])
            total = part if total is None else total + part
        for kd in range(3):
            hid[z + kd] = hid[z + kd] + total[kd * MID : (kd + 1) * MID]
    act[...] = jnp.zeros_like(act)
    for w in range(-1, Z + 1):
        for r in range(R):
            cols = slice(r * X, (r + 1) * X)
            scale = kept_scale(scal[2], scal[3], scal[0] + w, scal[1] + r)
            if not 0 <= w < Z:
                edge[0 if w < 0 else 1, :, cols] = scale.astype(BF16)
                continue
            hidden, kept = scaled(tile(got, PRE[w] + r), scale)
            act[(w + 1) * MID : (w + 2) * MID, cols] = hidden
            mask[w, :, cols] = kept.astype(BF16)
    for kh in range(3):
        total = None
        for s in range(Z):
            part = dot_t(g3[s, :, (2 - kh) * X : (4 - kh) * X], act[s * MID : (s + 3) * MID])
            total = part if total is None else total + part
        two[kh] = total
    order = shuffle(False)
    feat[...] = jnp.zeros_like(feat)
    for w in range(Z):
        for i in range(2):
            rows = dot(order, tile(got, FEAT + 2 * w + i).astype(BF16)).astype(BF16)
            for r in range(2):
                cols = slice((2 * i + r) * X, (2 * i + r + 1) * X)
                feat[(w + 2) * CIN : (w + 3) * CIN, cols] = rows[r * CIN : (r + 1) * CIN]
    for kd in range(3):
        for kh in range(3):
            for kw in range(3):
                at = (kd * 3 + kh) * CIN
                wf[at : at + CIN, kw * 128 : (kw + 1) * 128] = w_one[9 * kd + 3 * kh + kw]
    fin[...] = jnp.zeros_like(fin)
    for at, z in enumerate((1, 2)):
        for r in range(R):
            cols = slice(r * X, (r + 1) * X)
            store_shifts(p3, at, r, hid[z + 1, :, cols] * mask[z, :, cols].astype(F32))
        add_feature_terms(fin, wf, p3[at], z)
    for kh in range(3):
        one[kh] = raw_one_terms(feat, ((1, p3[0]), (2, p3[1])), None, kh)


def kernel_c(
    scal, halo_l, halo_r, g3, part_hid, mask, edge, part_two, wk, feat, wf, part_fin, part_one,
    fout, slabs, theirs, g, hid, act, p3, fin,
):
    core, has_l, has_r = scal[4], scal[5] > 0, scal[6] > 0
    slabs[:, 20:] = jnp.zeros((2, 4, 128, 128), F32)
    for at in range(4):
        for r in range(4):
            if at < 2:
                store_shifts(g, at, r, jnp.where(has_l, tile(halo_l, 4 * at + r), 0.0))
            else:
                store_shifts(g, at, r, jnp.where(has_r, tile(halo_r, 4 * at - 6 + r), 0.0))
    hid[...] = part_hid[...]
    for at, plane, first, end in ((0, -2, 2, 3), (1, -1, 1, 3), (2, 4, 0, 2), (3, 5, 0, 1)):
        total = None
        for kh in range(3):
            part = dot(wk[kh, first * MID : end * MID], g[at, :, (2 - kh) * X : (4 - kh) * X])
            total = part if total is None else total + part
        for kd in range(first, end):
            hid[plane + kd] = hid[plane + kd] + total[(kd - first) * MID : (kd - first + 1) * MID]
    outer = (-1, 0, Z - 1, Z)
    for at, plane in enumerate(outer):
        j = plane + 1
        for r in range(R):
            cols = slice(r * X, (r + 1) * X)
            if j == 0:
                hidden, kept = scaled(jnp.where(has_l, tile(halo_l, 8 + r), 0.0), edge[0, :, cols].astype(F32))
                act[0, :, cols] = hidden
            elif j == Z + 1:
                hidden, kept = scaled(jnp.where(has_r, tile(halo_r, r), 0.0), edge[1, :, cols].astype(F32))
                act[1, :, cols] = hidden
            else:
                kept = mask[j - 1, :, cols].astype(F32)
            store_shifts(p3, at, r, hid[j, :, cols] * kept)
    for kh in range(3):
        rows = slice((2 - kh) * X, (4 - kh) * X)
        low = dot_t(g3[0, :, rows], act[0])
        high = dot_t(g3[Z - 1, :, rows], act[1])
        for kd in range(3):
            for kw in range(3):
                slab = part_two[kh, kw * 128 : (kw + 1) * 128, kd * MID : (kd + 1) * MID]
                if kd != 1:
                    slab = slab + (low if kd == 0 else high)[kw * 128 : (kw + 1) * 128]
                store_slab(core, slabs, 9 * kd + 3 * kh + kw, slab)
    fin[...] = part_fin[...]
    for at, plane in enumerate(outer):
        add_feature_terms(fin, wf, p3[at], plane)
    last = []
    for kh in range(3):
        total = raw_one_terms(feat, [(plane, p3[at]) for at, plane in enumerate(outer)], part_one[kh], kh)
        for kw in range(3):
            store_slab(core, slabs, 27 + 3 * kh + kw, total[kw * 128 : (kw + 1) * 128, : 2 * CIN])
            last.append(total[kw * 128 : (kw + 1) * 128, 2 * CIN :])
    last.append(jnp.zeros((128, CIN), F32))
    for b in range(5):
        store_slab(core, slabs, 36 + b, jnp.concatenate([last[b], last[b + 5]], axis=1))
    back = shuffle(True)
    for w in range(Z):
        for i in range(2):
            rows = jnp.concatenate([fin[w, :, (2 * i + r) * X : (2 * i + r + 1) * X] for r in range(2)], axis=0)
            fout[:, 2 * w + i] = dot(back, rows.astype(BF16)).reshape(16, 8, X).astype(BF16)
    theirs[...] = slabs[1].astype(BF16)


def kernel_p(shares, feature, sent):
    for i in range(3):
        total = shares[0, i].astype(F32)
        for j in range(1, 8):
            total = total + shares[j, i].astype(F32)
        high = total.astype(BF16).astype(F32)
        sent[:, i] = high.reshape(16, 8, X).astype(BF16)
        sent[:, 3 + i] = (total - high).reshape(16, 8, X).astype(BF16)
    sent[:, 6:] = feature[...]


def kernel_q(got, copies):
    scale = 1.0 / math.sqrt(NZ * NY * X)
    total = got[0, :6].astype(F32)
    for j in range(1, 16):
        total = total + got[j, :6].astype(F32)
    total = (total[:3] + total[3:]) * scale
    for j in range(16):
        copies[j] = total


VMEM, SMEM = pl.BlockSpec(memory_space=pltpu.VMEM), pl.BlockSpec(memory_space=pltpu.SMEM)


def call(body, args, outs, scratch, flops, scalars):
    return pl.pallas_call(
        body,
        out_shape=tuple(jax.ShapeDtypeStruct(shape, kind) for shape, kind in outs),
        in_specs=[SMEM] * scalars + [VMEM] * (len(args) - scalars),
        out_specs=(VMEM,) * len(outs),
        scratch_shapes=[pltpu.VMEM(shape, kind) for shape, kind in scratch],
        compiler_params=pltpu.CompilerParams(vmem_limit_bytes=24 * 1024 * 1024),
        cost_estimate=pl.CostEstimate(flops=flops, bytes_accessed=4 * 1024 * 1024, transcendentals=0),
    )(*args)


def shards(features, pre_act, out_grad, weight_one, weight_two, dropout_seed, layer_offset):
    chan_pos, slab_pos, core = lax.axis_index(CHAN), lax.axis_index(SLAB), lax.axis_index("core")

    anywhere = pl.BlockSpec(memory_space=pl.ANY)
    sent = pl.pallas_call(
        kernel_s,
        out_shape=jax.ShapeDtypeStruct((16, 32, 8, X), BF16),
        in_specs=[anywhere] * 3,
        out_specs=VMEM,
        scratch_shapes=[
            pltpu.VMEM(out_grad.shape, BF16),
            pltpu.VMEM(pre_act.shape, BF16),
            pltpu.VMEM(features.shape, BF16),
            pltpu.VMEM((2 * Z, NY * 8, X), F32),
            pltpu.VMEM((Z, (NY + 2) * 4, X), F32),
            pltpu.SemaphoreType.DMA((3,)),
        ],
        compiler_params=pltpu.CompilerParams(vmem_limit_bytes=56 * 1024 * 1024),
    )(out_grad, pre_act, features)
    got = lax.all_to_all(sent, CHAN, 0, 0, tiled=True)

    up = [(i, (i + 1) % 16) for i in range(16)]
    down = [((i + 1) % 16, i) for i in range(16)]
    swap = [(0, 1), (1, 0)]
    halo_l = lax.ppermute(got[:, 10:20], SLAB, up)
    halo_r = lax.ppermute(got[:, :10], SLAB, down)
    has_l, has_r = slab_pos > 0, slab_pos < 15
    scal = jnp.stack(
        [slab_pos * Z, chan_pos * R, layer_offset[0], dropout_seed[0], core, has_l.astype(jnp.int32), has_r.astype(jnp.int32)]
    )

    own = call(
        kernel_a,
        (scal, got, weight_two, weight_one),
        [
            ((Z, 384, 4 * X), BF16),
            ((Z + 2, MID, R * X), F32),
            ((Z, MID, R * X), BF16),
            ((2, MID, R * X), BF16),
            ((3, 384, 384), F32),
            ((3, 384, 384), BF16),
            (((Z + 4) * CIN, 4 * X), BF16),
            ((9 * CIN, 384), BF16),
            ((Z, CIN, 4 * X), F32),
            ((3, 384, 3 * CIN), F32),
        ],
        [(((Z + 2) * MID, R * X), BF16), ((2, 384, R * X), BF16)],
        6 * 10**9,
        1,
    )
    feature, slabs, theirs = call(
        kernel_c,
        (scal, halo_l, halo_r) + tuple(own),
        [
            ((16, 8, 8, X), BF16),
            ((2, 24, 128, 128), F32),
            ((24, 128, 128), BF16),
        ],
        [
            ((4, 384, 4 * X), BF16),
            ((Z + 2, MID, R * X), F32),
            ((2, MID, R * X), BF16),
            ((4, 384, R * X), BF16),
            ((Z, CIN, 4 * X), F32),
        ],
        3 * 10**9,
        1,
    )

    mine = (slabs[0] + lax.ppermute(theirs, "core", swap).astype(F32)).astype(BF16)
    shares = lax.all_to_all(mine.reshape(8, 3, 128, 128), ("x", "zl"), 0, 0, tiled=True)
    (sent,) = call(kernel_p, (shares, feature), [((16, 14, 8, X), BF16)], [], 10**6, 0)
    got = lax.all_to_all(sent, CHAN, 0, 0, tiled=True)

    rows = got[:, 6:].astype(F32).reshape(16, Z, 4, 4, X)
    none = jnp.zeros((1, Z, 4, X), F32)
    first = rows[:, :, 1] + jnp.concatenate([none, rows[:-1, :, 3]])
    second = rows[:, :, 2] + jnp.concatenate([rows[1:, :, 0], none])
    feature = jnp.stack([first, second], axis=2).transpose(3, 1, 0, 2, 4).reshape(4, Z, NY, X)

    (copies,) = call(kernel_q, (got,), [((16, 3, 8, 128), F32)], [], 10**6, 0)
    total = lax.all_to_all(copies, SLAB, 0, 0, tiled=True)
    total = total.reshape(48, 8, 128)
    two, one = total[:27], total[27:41].reshape(14, 8, 2, CIN)
    one = jnp.concatenate([one[:9, :, 0], one[:9, :, 1], one[9:, :, 0], one[9:13, :, 1]])
    two = two.transpose(1, 2, 0).reshape(8, 27 * MID)
    one = one.transpose(1, 2, 0).reshape(4, 54 * CIN)
    return feature, one, two


def solution(mesh):
    split = Mesh(mesh.devices.reshape(4, 2, 2, 4, 4), ("x", "zl", "core", "y", "zh"))
    cells = P(CHAN, SLAB, None, None)
    return jax.shard_map(
        shards,
        mesh=split,
        in_specs=(cells, cells, cells, P(), P(), P(), P()),
        out_specs=(cells, P(CHAN, None), P(CHAN, None)),
        check_vma=False,
    )
```

```python
import math

import jax
import jax.numpy as jnp
from jax import lax
from jax.experimental import pallas as pl
from jax.experimental.pallas import tpu as pltpu
from jax.sharding import Mesh
from jax.sharding import PartitionSpec as P

BF16, F32 = jnp.bfloat16, jnp.float32
CHAN, SLAB = ("y", "zh"), ("x", "zl", "core")
Z, R, X = 4, 2, 128
NZ, NY = 64, 32
MID, CIN = 128, 64
PRE, GRAD, FEAT = (0, 20, 22, 18), 2, 24


def kept_scale(offset, seed, z, h):
    c = lax.broadcasted_iota(jnp.int32, (MID, X), 0)
    w = lax.broadcasted_iota(jnp.int32, (MID, X), 1)
    position = ((c * NZ + z) * NY + h) * X + w
    m = (position + offset) ^ seed
    m = m * jnp.int32(739982445)
    m = m ^ lax.shift_right_logical(m, jnp.int32(15))
    m = m * jnp.int32(695938361)
    m = m ^ lax.shift_right_logical(m, jnp.int32(12))
    return jnp.where((m & 65535) < 52429, F32(1.25), F32(0.0))


def store_shifts(dst, plane, row, block):
    lane = lax.broadcasted_iota(jnp.int32, block.shape, 1)
    cols = slice(row * X, (row + 1) * X)
    ahead = jnp.where(lane == X - 1, 0.0, pltpu.roll(block, X - 1, 1))
    behind = jnp.where(lane == 0, 0.0, pltpu.roll(block, 1, 1))
    dst[plane, 0:128, cols] = ahead.astype(BF16)
    dst[plane, 128:256, cols] = block.astype(BF16)
    dst[plane, 256:384, cols] = behind.astype(BF16)


def dot(a, b):
    return lax.dot_general(a, b, (((1,), (0,)), ((), ())), preferred_element_type=F32)


def dot_t(a, b):
    return lax.dot_general(a, b, (((1,), (1,)), ((), ())), preferred_element_type=F32)


def tile(ref, t):
    return ref[:, t].astype(F32).reshape(128, X)


def store_slab(core, slabs, s, slab):
    slabs[core ^ (s // 3 % 2), s // 6 * 3 + s % 3] = slab


def shuffle(back):
    i = lax.broadcasted_iota(jnp.int32, (128, 128), 1 if back else 0)
    j = lax.broadcasted_iota(jnp.int32, (128, 128), 0 if back else 1)
    at = (lax.rem(i, 64) // 4) * 8 + (i // 64) * 4 + lax.rem(i, 4)
    return jnp.where(at == j, F32(1.0), F32(0.0)).astype(BF16)


def scaled(pre, scale):
    return (jnp.maximum(pre, 0.0) * scale).astype(BF16), jnp.where(pre > 0, scale, 0.0)


def kernel_s(grad_in, pre_in, feat_in, out, sent, grad, pre, feat, rows8, rows4, sems):
    copies = [
        pltpu.make_async_copy(src, dst, sems.at[i])
        for i, (src, dst) in enumerate(((grad_in, grad), (pre_in, pre), (feat_in, feat)))
    ]
    for copy in copies:
        copy.start()
    sent[0, GRAD : GRAD + 4 * Z] = jnp.zeros((4 * Z, 8, X), BF16)
    sent[15, GRAD : GRAD + 4 * Z] = jnp.zeros((4 * Z, 8, X), BF16)
    rows4[...] = jnp.zeros_like(rows4)
    copies[0].wait()
    for z in range(Z):
        for c in range(8):
            rows8[z, pl.ds(c, NY, stride=8), :] = grad[c, z].astype(F32)
        rows = rows8[z].reshape(16, 2, 8, X).astype(BF16)
        at = GRAD + 4 * z
        sent[1:, at] = rows[:-1, 1]
        sent[:, at + 1] = rows[:, 0]
        sent[:, at + 2] = rows[:, 1]
        sent[:-1, at + 3] = rows[1:, 0]
    copies[1].wait()
    for z in range(Z):
        for c in range(8):
            rows8[Z + z, pl.ds(c, NY, stride=8), :] = pre[c, z].astype(F32)
        rows = rows8[Z + z].reshape(16, 2, 8, X).astype(BF16)
        sent[:, PRE[z]] = rows[:, 0]
        sent[:, PRE[z] + 1] = rows[:, 1]
    first = pltpu.make_async_copy(sent.at[:, :FEAT], out.at[:, :FEAT], sems.at[3])
    first.start()
    copies[2].wait()
    for z in range(Z):
        for c in range(4):
            rows4[z, pl.ds(4 + c, NY, stride=4), :] = feat[c, z].astype(F32)
        rows = rows4[z].reshape(17, 8, X).astype(BF16)
        sent[:, FEAT + 2 * z] = rows[:-1]
        sent[:, FEAT + 2 * z + 1] = rows[1:]
    last = pltpu.make_async_copy(sent.at[:, FEAT:], out.at[:, FEAT:], sems.at[4])
    last.start()
    first.wait()
    last.wait()


def add_feature_terms(fin, wf, rows, plane):
    first, end = max(0, 1 - plane), min(3, Z + 1 - plane)
    terms = dot(wf[first * 3 * CIN : end * 3 * CIN], rows)
    for kd in range(first, end):
        for kh in range(3):
            at = ((kd - first) * 3 + kh) * CIN
            cols = slice(kh * X, (kh + 2) * X)
            fin[plane - 1 + kd, :, cols] = fin[plane - 1 + kd, :, cols] + terms[at : at + CIN]


def raw_one_terms(feat, planes, total, kh):
    for plane, rows in planes:
        part = dot_t(rows, feat[(plane + 1) * CIN : (plane + 4) * CIN, kh * X : (kh + 2) * X])
        total = part if total is None else total + part
    return total


def kernel_a(scal, got, w_two, w_one, g3, hid, mask, edge, two, wk, feat, wf, fin, one, act, p3):
    for kd in range(3):
        for kh in range(3):
            for kw in range(3):
                wk[kh, kd * MID : (kd + 1) * MID, kw * 128 : (kw + 1) * 128] = w_two[9 * kd + 3 * kh + kw]
    for z in range(Z):
        for r in range(4):
            store_shifts(g3, z, r, tile(got, GRAD + 4 * z + r))
    hid[...] = jnp.zeros_like(hid)
    for z in range(Z):
        total = None
        for kh in range(3):
            part = dot(wk[kh], g3[z, :, (2 - kh) * X : (4 - kh) * X])
            total = part if total is None else total + part
        for kd in range(3):
            hid[z + kd] = hid[z + kd] + total[kd * MID : (kd + 1) * MID]
    act[...] = jnp.zeros_like(act)
    for w in range(-1, Z + 1):
        for r in range(R):
            cols = slice(r * X, (r + 1) * X)
            scale = kept_scale(scal[2], scal[3], scal[0] + w, scal[1] + r)
            if not 0 <= w < Z:
                edge[0 if w < 0 else 1, :, cols] = scale.astype(BF16)
                continue
            hidden, kept = scaled(tile(got, PRE[w] + r), scale)
            act[(w + 1) * MID : (w + 2) * MID, cols] = hidden
            mask[w, :, cols] = kept.astype(BF16)
    for kh in range(3):
        total = None
        for s in range(Z):
            part = dot_t(g3[s, :, (2 - kh) * X : (4 - kh) * X], act[s * MID : (s + 3) * MID])
            total = part if total is None else total + part
        two[kh] = total
    order = shuffle(False)
    feat[...] = jnp.zeros_like(feat)
    for w in range(Z):
        for i in range(2):
            rows = dot(order, tile(got, FEAT + 2 * w + i).astype(BF16)).astype(BF16)
            for r in range(2):
                cols = slice((2 * i + r) * X, (2 * i + r + 1) * X)
                feat[(w + 2) * CIN : (w + 3) * CIN, cols] = rows[r * CIN : (r + 1) * CIN]
    for kd in range(3):
        for kh in range(3):
            for kw in range(3):
                at = (kd * 3 + kh) * CIN
                wf[at : at + CIN, kw * 128 : (kw + 1) * 128] = w_one[9 * kd + 3 * kh + kw]
    fin[...] = jnp.zeros_like(fin)
    for at, z in enumerate((1, 2)):
        for r in range(R):
            cols = slice(r * X, (r + 1) * X)
            store_shifts(p3, at, r, hid[z + 1, :, cols] * mask[z, :, cols].astype(F32))
        add_feature_terms(fin, wf, p3[at], z)
    for kh in range(3):
        one[kh] = raw_one_terms(feat, ((1, p3[0]), (2, p3[1])), None, kh)


def kernel_c(
    scal, halo_l, halo_r, g3, part_hid, mask, edge, part_two, wk, feat, wf, part_fin, part_one,
    fout, slabs, theirs, g, hid, act, p3, fin,
):
    core, has_l, has_r = scal[4], scal[5] > 0, scal[6] > 0
    slabs[:, 20:] = jnp.zeros((2, 4, 128, 128), F32)
    for at in range(4):
        for r in range(4):
            if at < 2:
                store_shifts(g, at, r, jnp.where(has_l, tile(halo_l, 4 * at + r), 0.0))
            else:
                store_shifts(g, at, r, jnp.where(has_r, tile(halo_r, 4 * at - 6 + r), 0.0))
    hid[...] = part_hid[...]
    for at, plane, first, end in ((0, -2, 2, 3), (1, -1, 1, 3), (2, 4, 0, 2), (3, 5, 0, 1)):
        total = None
        for kh in range(3):
            part = dot(wk[kh, first * MID : end * MID], g[at, :, (2 - kh) * X : (4 - kh) * X])
            total = part if total is None else total + part
        for kd in range(first, end):
            hid[plane + kd] = hid[plane + kd] + total[(kd - first) * MID : (kd - first + 1) * MID]
    outer = (-1, 0, Z - 1, Z)
    for at, plane in enumerate(outer):
        j = plane + 1
        for r in range(R):
            cols = slice(r * X, (r + 1) * X)
            if j == 0:
                hidden, kept = scaled(jnp.where(has_l, tile(halo_l, 8 + r), 0.0), edge[0, :, cols].astype(F32))
                act[0, :, cols] = hidden
            elif j == Z + 1:
                hidden, kept = scaled(jnp.where(has_r, tile(halo_r, r), 0.0), edge[1, :, cols].astype(F32))
                act[1, :, cols] = hidden
            else:
                kept = mask[j - 1, :, cols].astype(F32)
            store_shifts(p3, at, r, hid[j, :, cols] * kept)
    for kh in range(3):
        rows = slice((2 - kh) * X, (4 - kh) * X)
        low = dot_t(g3[0, :, rows], act[0])
        high = dot_t(g3[Z - 1, :, rows], act[1])
        for kd in range(3):
            for kw in range(3):
                slab = part_two[kh, kw * 128 : (kw + 1) * 128, kd * MID : (kd + 1) * MID]
                if kd != 1:
                    slab = slab + (low if kd == 0 else high)[kw * 128 : (kw + 1) * 128]
                store_slab(core, slabs, 9 * kd + 3 * kh + kw, slab)
    fin[...] = part_fin[...]
    for at, plane in enumerate(outer):
        add_feature_terms(fin, wf, p3[at], plane)
    last = []
    for kh in range(3):
        total = raw_one_terms(feat, [(plane, p3[at]) for at, plane in enumerate(outer)], part_one[kh], kh)
        for kw in range(3):
            store_slab(core, slabs, 27 + 3 * kh + kw, total[kw * 128 : (kw + 1) * 128, : 2 * CIN])
            last.append(total[kw * 128 : (kw + 1) * 128, 2 * CIN :])
    last.append(jnp.zeros((128, CIN), F32))
    for b in range(5):
        store_slab(core, slabs, 36 + b, jnp.concatenate([last[b], last[b + 5]], axis=1))
    back = shuffle(True)
    for w in range(Z):
        for i in range(2):
            rows = jnp.concatenate([fin[w, :, (2 * i + r) * X : (2 * i + r + 1) * X] for r in range(2)], axis=0)
            fout[:, 2 * w + i] = dot(back, rows.astype(BF16)).reshape(16, 8, X).astype(BF16)
    theirs[...] = slabs[1].astype(BF16)


def kernel_p(shares, feature, sent):
    for i in range(3):
        total = shares[0, i].astype(F32)
        for j in range(1, 8):
            total = total + shares[j, i].astype(F32)
        high = total.astype(BF16).astype(F32)
        sent[:, i] = high.reshape(16, 8, X).astype(BF16)
        sent[:, 3 + i] = (total - high).reshape(16, 8, X).astype(BF16)
    sent[:, 6:] = feature[...]


def kernel_q(got, copies):
    scale = 1.0 / math.sqrt(NZ * NY * X)
    total = got[0, :6].astype(F32)
    for j in range(1, 16):
        total = total + got[j, :6].astype(F32)
    total = (total[:3] + total[3:]) * scale
    for j in range(16):
        copies[j] = total


VMEM, SMEM = pl.BlockSpec(memory_space=pltpu.VMEM), pl.BlockSpec(memory_space=pltpu.SMEM)


def call(body, args, outs, scratch, flops, scalars):
    return pl.pallas_call(
        body,
        out_shape=tuple(jax.ShapeDtypeStruct(shape, kind) for shape, kind in outs),
        in_specs=[SMEM] * scalars + [VMEM] * (len(args) - scalars),
        out_specs=(VMEM,) * len(outs),
        scratch_shapes=[pltpu.VMEM(shape, kind) for shape, kind in scratch],
        compiler_params=pltpu.CompilerParams(vmem_limit_bytes=24 * 1024 * 1024),
        cost_estimate=pl.CostEstimate(flops=flops, bytes_accessed=4 * 1024 * 1024, transcendentals=0),
    )(*args)


def shards(features, pre_act, out_grad, weight_one, weight_two, dropout_seed, layer_offset):
    chan_pos, slab_pos, core = lax.axis_index(CHAN), lax.axis_index(SLAB), lax.axis_index("core")

    anywhere = pl.BlockSpec(memory_space=pl.ANY)
    sent = pl.pallas_call(
        kernel_s,
        out_shape=jax.ShapeDtypeStruct((16, 32, 8, X), BF16),
        in_specs=[anywhere] * 3,
        out_specs=anywhere,
        scratch_shapes=[
            pltpu.VMEM((16, 32, 8, X), BF16),
            pltpu.VMEM(out_grad.shape, BF16),
            pltpu.VMEM(pre_act.shape, BF16),
            pltpu.VMEM(features.shape, BF16),
            pltpu.VMEM((2 * Z, NY * 8, X), F32),
            pltpu.VMEM((Z, (NY + 2) * 4, X), F32),
            pltpu.SemaphoreType.DMA((5,)),
        ],
        compiler_params=pltpu.CompilerParams(vmem_limit_bytes=56 * 1024 * 1024),
    )(out_grad, pre_act, features)
    got = lax.all_to_all(sent, CHAN, 0, 0, tiled=True)

    up = [(i, (i + 1) % 16) for i in range(16)]
    down = [((i + 1) % 16, i) for i in range(16)]
    swap = [(0, 1), (1, 0)]
    halo_l = lax.ppermute(got[:, 10:20], SLAB, up)
    halo_r = lax.ppermute(got[:, :10], SLAB, down)
    has_l, has_r = slab_pos > 0, slab_pos < 15
    scal = jnp.stack(
        [slab_pos * Z, chan_pos * R, layer_offset[0], dropout_seed[0], core, has_l.astype(jnp.int32), has_r.astype(jnp.int32)]
    )

    own = call(
        kernel_a,
        (scal, got, weight_two, weight_one),
        [
            ((Z, 384, 4 * X), BF16),
            ((Z + 2, MID, R * X), F32),
            ((Z, MID, R * X), BF16),
            ((2, MID, R * X), BF16),
            ((3, 384, 384), F32),
            ((3, 384, 384), BF16),
            (((Z + 4) * CIN, 4 * X), BF16),
            ((9 * CIN, 384), BF16),
            ((Z, CIN, 4 * X), F32),
            ((3, 384, 3 * CIN), F32),
        ],
        [(((Z + 2) * MID, R * X), BF16), ((2, 384, R * X), BF16)],
        6 * 10**9,
        1,
    )
    feature, slabs, theirs = call(
        kernel_c,
        (scal, halo_l, halo_r) + tuple(own),
        [
            ((16, 8, 8, X), BF16),
            ((2, 24, 128, 128), F32),
            ((24, 128, 128), BF16),
        ],
        [
            ((4, 384, 4 * X), BF16),
            ((Z + 2, MID, R * X), F32),
            ((2, MID, R * X), BF16),
            ((4, 384, R * X), BF16),
            ((Z, CIN, 4 * X), F32),
        ],
        3 * 10**9,
        1,
    )

    mine = (slabs[0] + lax.ppermute(theirs, "core", swap).astype(F32)).astype(BF16)
    shares = lax.all_to_all(mine.reshape(8, 3, 128, 128), ("x", "zl"), 0, 0, tiled=True)
    (sent,) = call(kernel_p, (shares, feature), [((16, 14, 8, X), BF16)], [], 10**6, 0)
    got = lax.all_to_all(sent, CHAN, 0, 0, tiled=True)

    rows = got[:, 6:].astype(F32).reshape(16, Z, 4, 4, X)
    none = jnp.zeros((1, Z, 4, X), F32)
    first = rows[:, :, 1] + jnp.concatenate([none, rows[:-1, :, 3]])
    second = rows[:, :, 2] + jnp.concatenate([rows[1:, :, 0], none])
    feature = jnp.stack([first, second], axis=2).transpose(3, 1, 0, 2, 4).reshape(4, Z, NY, X)

    (copies,) = call(kernel_q, (got,), [((16, 3, 8, 128), F32)], [], 10**6, 0)
    total = lax.all_to_all(copies, SLAB, 0, 0, tiled=True)
    total = total.reshape(48, 8, 128)
    two, one = total[:27], total[27:41].reshape(14, 8, 2, CIN)
    one = jnp.concatenate([one[:9, :, 0], one[:9, :, 1], one[9:, :, 0], one[9:13, :, 1]])
    two = two.transpose(1, 2, 0).reshape(8, 27 * MID)
    one = one.transpose(1, 2, 0).reshape(4, 54 * CIN)
    return feature, one, two


def solution(mesh):
    split = Mesh(mesh.devices.reshape(4, 2, 2, 4, 4), ("x", "zl", "core", "y", "zh"))
    cells = P(CHAN, SLAB, None, None)
    return jax.shard_map(
        shards,
        mesh=split,
        in_specs=(cells, cells, cells, P(), P(), P(), P()),
        out_specs=(cells, P(CHAN, None), P(CHAN, None)),
        check_vma=False,
    )
```

```python
import math

import jax
import jax.numpy as jnp
from jax import lax
from jax.experimental import pallas as pl
from jax.experimental.pallas import tpu as pltpu
from jax.sharding import Mesh
from jax.sharding import PartitionSpec as P

BF16, F32 = jnp.bfloat16, jnp.float32
CHAN, SLAB = ("y", "zh"), ("x", "zl", "core")
Z, R, X = 4, 2, 128
NZ, NY = 64, 32
MID, CIN = 128, 64
PRE, GRAD, FEAT = (0, 20, 22, 18), 2, 24


def kept_scale(offset, seed, z, h):
    c = lax.broadcasted_iota(jnp.int32, (MID, X), 0)
    w = lax.broadcasted_iota(jnp.int32, (MID, X), 1)
    position = ((c * NZ + z) * NY + h) * X + w
    m = (position + offset) ^ seed
    m = m * jnp.int32(739982445)
    m = m ^ lax.shift_right_logical(m, jnp.int32(15))
    m = m * jnp.int32(695938361)
    m = m ^ lax.shift_right_logical(m, jnp.int32(12))
    return jnp.where((m & 65535) < 52429, F32(1.25), F32(0.0))


def store_shifts(dst, plane, row, block):
    lane = lax.broadcasted_iota(jnp.int32, block.shape, 1)
    cols = slice(row * X, (row + 1) * X)
    ahead = jnp.where(lane == X - 1, 0.0, pltpu.roll(block, X - 1, 1))
    behind = jnp.where(lane == 0, 0.0, pltpu.roll(block, 1, 1))
    dst[plane, 0:128, cols] = ahead.astype(BF16)
    dst[plane, 128:256, cols] = block.astype(BF16)
    dst[plane, 256:384, cols] = behind.astype(BF16)


def dot(a, b):
    return lax.dot_general(a, b, (((1,), (0,)), ((), ())), preferred_element_type=F32)


def dot_t(a, b):
    return lax.dot_general(a, b, (((1,), (1,)), ((), ())), preferred_element_type=F32)


def tile(ref, t):
    return ref[:, t].astype(F32).reshape(128, X)


def store_slab(core, slabs, s, slab):
    slabs[core ^ (s // 3 % 2), s // 6 * 3 + s % 3] = slab


def shuffle(back):
    i = lax.broadcasted_iota(jnp.int32, (128, 128), 1 if back else 0)
    j = lax.broadcasted_iota(jnp.int32, (128, 128), 0 if back else 1)
    at = (lax.rem(i, 64) // 4) * 8 + (i // 64) * 4 + lax.rem(i, 4)
    return jnp.where(at == j, F32(1.0), F32(0.0)).astype(BF16)


def scaled(pre, scale):
    return (jnp.maximum(pre, 0.0) * scale).astype(BF16), jnp.where(pre > 0, scale, 0.0)


def kernel_s(grad_in, pre_in, feat_in, sent, grad, pre, feat, rows8, rows4, sems):
    copies = [
        pltpu.make_async_copy(src, dst, sems.at[i])
        for i, (src, dst) in enumerate(((grad_in, grad), (pre_in, pre), (feat_in, feat)))
    ]
    for copy in copies:
        copy.start()
    sent[0, GRAD : GRAD + 4 * Z] = jnp.zeros((4 * Z, 8, X), BF16)
    sent[15, GRAD : GRAD + 4 * Z] = jnp.zeros((4 * Z, 8, X), BF16)
    rows4[...] = jnp.zeros_like(rows4)
    copies[0].wait()
    for z in range(Z):
        for c in range(8):
            rows8[z, pl.ds(c, NY, stride=8), :] = grad[c, z].astype(F32)
        rows = rows8[z].reshape(16, 2, 8, X).astype(BF16)
        at = GRAD + 4 * z
        sent[1:, at] = rows[:-1, 1]
        sent[:, at + 1] = rows[:, 0]
        sent[:, at + 2] = rows[:, 1]
        sent[:-1, at + 3] = rows[1:, 0]
    copies[1].wait()
    copies[2].wait()
    for z in range(Z):
        for c in range(8):
            rows8[Z + z, pl.ds(c, NY, stride=8), :] = pre[c, z].astype(F32)
        rows = rows8[Z + z].reshape(16, 2, 8, X).astype(BF16)
        sent[:, PRE[z]] = rows[:, 0]
        sent[:, PRE[z] + 1] = rows[:, 1]
        for c in range(4):
            rows4[z, pl.ds(4 + c, NY, stride=4), :] = feat[c, z].astype(F32)
        rows = rows4[z].reshape(17, 8, X).astype(BF16)
        sent[:, FEAT + 2 * z] = rows[:-1]
        sent[:, FEAT + 2 * z + 1] = rows[1:]


def add_feature_terms(fin, wf, rows, plane):
    first, end = max(0, 1 - plane), min(3, Z + 1 - plane)
    terms = dot(wf[first * 3 * CIN : end * 3 * CIN], rows)
    for kd in range(first, end):
        for kh in range(3):
            at = ((kd - first) * 3 + kh) * CIN
            cols = slice(kh * X, (kh + 2) * X)
            fin[plane - 1 + kd, :, cols] = fin[plane - 1 + kd, :, cols] + terms[at : at + CIN]


def raw_one_terms(feat, planes, total, kh):
    for plane, rows in planes:
        part = dot_t(rows, feat[(plane + 1) * CIN : (plane + 4) * CIN, kh * X : (kh + 2) * X])
        total = part if total is None else total + part
    return total


def kernel_a(scal, got, w_two, w_one, g3, hid, mask, edge, two, wk, feat, wf, fin, one, act, p3):
    for kd in range(3):
        for kh in range(3):
            for kw in range(3):
                wk[kh, kd * MID : (kd + 1) * MID, kw * 128 : (kw + 1) * 128] = w_two[9 * kd + 3 * kh + kw]
    for z in range(Z):
        for r in range(4):
            store_shifts(g3, z, r, tile(got, GRAD + 4 * z + r))
    hid[...] = jnp.zeros_like(hid)
    for z in range(Z):
        total = None
        for kh in range(3):
            part = dot(wk[kh], g3[z, :, (2 - kh) * X : (4 - kh) * X])
            total = part if total is None else total + part
        for kd in range(3):
            hid[z + kd] = hid[z + kd] + total[kd * MID : (kd + 1) * MID]
    act[...] = jnp.zeros_like(act)
    for w in range(-1, Z + 1):
        for r in range(R):
            cols = slice(r * X, (r + 1) * X)
            scale = kept_scale(scal[2], scal[3], scal[0] + w, scal[1] + r)
            if not 0 <= w < Z:
                edge[0 if w < 0 else 1, :, cols] = scale.astype(BF16)
                continue
            hidden, kept = scaled(tile(got, PRE[w] + r), scale)
            act[(w + 1) * MID : (w + 2) * MID, cols] = hidden
            mask[w, :, cols] = kept.astype(BF16)
    for kh in range(3):
        total = None
        for s in range(Z):
            part = dot_t(g3[s, :, (2 - kh) * X : (4 - kh) * X], act[s * MID : (s + 3) * MID])
            total = part if total is None else total + part
        two[kh] = total
    order = shuffle(False)
    feat[...] = jnp.zeros_like(feat)
    for w in range(Z):
        for i in range(2):
            rows = dot(order, tile(got, FEAT + 2 * w + i).astype(BF16)).astype(BF16)
            for r in range(2):
                cols = slice((2 * i + r) * X, (2 * i + r + 1) * X)
                feat[(w + 2) * CIN : (w + 3) * CIN, cols] = rows[r * CIN : (r + 1) * CIN]
    for kd in range(3):
        for kh in range(3):
            for kw in range(3):
                at = (kd * 3 + kh) * CIN
                wf[at : at + CIN, kw * 128 : (kw + 1) * 128] = w_one[9 * kd + 3 * kh + kw]
    fin[...] = jnp.zeros_like(fin)
    for at, z in enumerate((1, 2)):
        for r in range(R):
            cols = slice(r * X, (r + 1) * X)
            store_shifts(p3, at, r, hid[z + 1, :, cols] * mask[z, :, cols].astype(F32))
        add_feature_terms(fin, wf, p3[at], z)
    for kh in range(3):
        one[kh] = raw_one_terms(feat, ((1, p3[0]), (2, p3[1])), None, kh)


def kernel_c(
    scal, halo_l, halo_r, g3, part_hid, mask, edge, part_two, wk, feat, wf, part_fin, part_one,
    fout, slabs, theirs, g, hid, act, p3, fin,
):
    core, has_l, has_r = scal[4], scal[5] > 0, scal[6] > 0
    slabs[:, 20:] = jnp.zeros((2, 1, 128, 128), F32)
    for at in range(4):
        for r in range(4):
            if at < 2:
                store_shifts(g, at, r, jnp.where(has_l, tile(halo_l, 4 * at + r), 0.0))
            else:
                store_shifts(g, at, r, jnp.where(has_r, tile(halo_r, 4 * at - 6 + r), 0.0))
    hid[0:2] = part_hid[0:2]
    hid[Z:] = part_hid[Z:]
    for at, plane, first, end in ((0, -2, 2, 3), (1, -1, 1, 3), (2, 4, 0, 2), (3, 5, 0, 1)):
        total = None
        for kh in range(3):
            part = dot(wk[kh, first * MID : end * MID], g[at, :, (2 - kh) * X : (4 - kh) * X])
            total = part if total is None else total + part
        for kd in range(first, end):
            hid[plane + kd] = hid[plane + kd] + total[(kd - first) * MID : (kd - first + 1) * MID]
    outer = (-1, 0, Z - 1, Z)
    for at, plane in enumerate(outer):
        j = plane + 1
        for r in range(R):
            cols = slice(r * X, (r + 1) * X)
            if j == 0:
                hidden, kept = scaled(jnp.where(has_l, tile(halo_l, 8 + r), 0.0), edge[0, :, cols].astype(F32))
                act[0, :, cols] = hidden
            elif j == Z + 1:
                hidden, kept = scaled(jnp.where(has_r, tile(halo_r, r), 0.0), edge[1, :, cols].astype(F32))
                act[1, :, cols] = hidden
            else:
                kept = mask[j - 1, :, cols].astype(F32)
            store_shifts(p3, at, r, hid[j, :, cols] * kept)
    for kh in range(3):
        rows = slice((2 - kh) * X, (4 - kh) * X)
        low = dot_t(g3[0, :, rows], act[0])
        high = dot_t(g3[Z - 1, :, rows], act[1])
        for kd in range(3):
            for kw in range(3):
                slab = part_two[kh, kw * 128 : (kw + 1) * 128, kd * MID : (kd + 1) * MID]
                if kd != 1:
                    slab = slab + (low if kd == 0 else high)[kw * 128 : (kw + 1) * 128]
                store_slab(core, slabs, 9 * kd + 3 * kh + kw, slab)
    fin[...] = part_fin[...]
    for at, plane in enumerate(outer):
        add_feature_terms(fin, wf, p3[at], plane)
    last = []
    for kh in range(3):
        total = raw_one_terms(feat, [(plane, p3[at]) for at, plane in enumerate(outer)], part_one[kh], kh)
        for kw in range(3):
            store_slab(core, slabs, 27 + 3 * kh + kw, total[kw * 128 : (kw + 1) * 128, : 2 * CIN])
            last.append(total[kw * 128 : (kw + 1) * 128, 2 * CIN :])
    last.append(jnp.zeros((128, CIN), F32))
    for b in range(5):
        store_slab(core, slabs, 36 + b, jnp.concatenate([last[b], last[b + 5]], axis=1))
    back = shuffle(True)
    for w in range(Z):
        for i in range(2):
            rows = jnp.concatenate([fin[w, :, (2 * i + r) * X : (2 * i + r + 1) * X] for r in range(2)], axis=0)
            fout[:, 2 * w + i] = dot(back, rows.astype(BF16)).reshape(16, 8, X).astype(BF16)
    theirs[...] = slabs[1].astype(BF16)


def kernel_p(shares, feature, sent):
    for i in range(3):
        total = shares[0, i].astype(F32)
        for j in range(1, 8):
            total = total + shares[j, i].astype(F32)
        high = total.astype(BF16).astype(F32)
        sent[:, i] = high.reshape(16, 8, X).astype(BF16)
        sent[:, 3 + i] = (total - high).reshape(16, 8, X).astype(BF16)
    sent[:, 6:] = feature[...]


def kernel_q(got, copies):
    scale = 1.0 / math.sqrt(NZ * NY * X)
    total = got[0, :6].astype(F32)
    for j in range(1, 16):
        total = total + got[j, :6].astype(F32)
    total = (total[:3] + total[3:]) * scale
    for j in range(16):
        copies[j] = total


VMEM, SMEM = pl.BlockSpec(memory_space=pltpu.VMEM), pl.BlockSpec(memory_space=pltpu.SMEM)


def call(body, args, outs, scratch, flops, scalars):
    return pl.pallas_call(
        body,
        out_shape=tuple(jax.ShapeDtypeStruct(shape, kind) for shape, kind in outs),
        in_specs=[SMEM] * scalars + [VMEM] * (len(args) - scalars),
        out_specs=(VMEM,) * len(outs),
        scratch_shapes=[pltpu.VMEM(shape, kind) for shape, kind in scratch],
        compiler_params=pltpu.CompilerParams(vmem_limit_bytes=24 * 1024 * 1024),
        cost_estimate=pl.CostEstimate(flops=flops, bytes_accessed=4 * 1024 * 1024, transcendentals=0),
    )(*args)


def shards(features, pre_act, out_grad, weight_one, weight_two, dropout_seed, layer_offset):
    chan_pos, slab_pos, core = lax.axis_index(CHAN), lax.axis_index(SLAB), lax.axis_index("core")

    anywhere = pl.BlockSpec(memory_space=pl.ANY)
    sent = pl.pallas_call(
        kernel_s,
        out_shape=jax.ShapeDtypeStruct((16, 32, 8, X), BF16),
        in_specs=[anywhere] * 3,
        out_specs=VMEM,
        scratch_shapes=[
            pltpu.VMEM(out_grad.shape, BF16),
            pltpu.VMEM(pre_act.shape, BF16),
            pltpu.VMEM(features.shape, BF16),
            pltpu.VMEM((2 * Z, NY * 8, X), F32),
            pltpu.VMEM((Z, (NY + 2) * 4, X), F32),
            pltpu.SemaphoreType.DMA((3,)),
        ],
        compiler_params=pltpu.CompilerParams(vmem_limit_bytes=56 * 1024 * 1024),
    )(out_grad, pre_act, features)
    got = lax.all_to_all(sent, CHAN, 0, 0, tiled=True)

    up = [(i, (i + 1) % 16) for i in range(16)]
    down = [((i + 1) % 16, i) for i in range(16)]
    swap = [(0, 1), (1, 0)]
    halo_l = lax.ppermute(got[:, 10:20], SLAB, up)
    halo_r = lax.ppermute(got[:, :10], SLAB, down)
    has_l, has_r = slab_pos > 0, slab_pos < 15
    scal = jnp.stack(
        [slab_pos * Z, chan_pos * R, layer_offset[0], dropout_seed[0], core, has_l.astype(jnp.int32), has_r.astype(jnp.int32)]
    )

    own = call(
        kernel_a,
        (scal, got, weight_two, weight_one),
        [
            ((Z, 384, 4 * X), BF16),
            ((Z + 2, MID, R * X), F32),
            ((Z, MID, R * X), BF16),
            ((2, MID, R * X), BF16),
            ((3, 384, 384), F32),
            ((3, 384, 384), BF16),
            (((Z + 4) * CIN, 4 * X), BF16),
            ((9 * CIN, 384), BF16),
            ((Z, CIN, 4 * X), F32),
            ((3, 384, 3 * CIN), F32),
        ],
        [(((Z + 2) * MID, R * X), BF16), ((2, 384, R * X), BF16)],
        6 * 10**9,
        1,
    )
    feature, slabs, theirs = call(
        kernel_c,
        (scal, halo_l, halo_r) + tuple(own),
        [
            ((16, 8, 8, X), BF16),
            ((2, 21, 128, 128), F32),
            ((21, 128, 128), BF16),
        ],
        [
            ((4, 384, 4 * X), BF16),
            ((Z + 2, MID, R * X), F32),
            ((2, MID, R * X), BF16),
            ((4, 384, R * X), BF16),
            ((Z, CIN, 4 * X), F32),
        ],
        3 * 10**9,
        1,
    )

    mine = (slabs[0] + lax.ppermute(theirs, "core", swap).astype(F32)).astype(BF16)
    mine = jnp.concatenate([mine, jnp.zeros((3, 128, 128), BF16)])
    shares = lax.all_to_all(mine.reshape(8, 3, 128, 128), ("x", "zl"), 0, 0, tiled=True)
    (sent,) = call(kernel_p, (shares, feature), [((16, 14, 8, X), BF16)], [], 10**6, 0)
    got = lax.all_to_all(sent, CHAN, 0, 0, tiled=True)

    rows = got[:, 6:].astype(F32).reshape(16, Z, 4, 4, X)
    none = jnp.zeros((1, Z, 4, X), F32)
    first = rows[:, :, 1] + jnp.concatenate([none, rows[:-1, :, 3]])
    second = rows[:, :, 2] + jnp.concatenate([rows[1:, :, 0], none])
    feature = jnp.stack([first, second], axis=2).transpose(3, 1, 0, 2, 4).reshape(4, Z, NY, X)

    (copies,) = call(kernel_q, (got,), [((16, 3, 8, 128), F32)], [], 10**6, 0)
    total = lax.all_to_all(copies, SLAB, 0, 0, tiled=True)
    total = total.reshape(48, 8, 128)
    two, one = total[:27], total[27:41].reshape(14, 8, 2, CIN)
    one = jnp.concatenate([one[:9, :, 0], one[:9, :, 1], one[9:, :, 0], one[9:13, :, 1]])
    two = two.transpose(1, 2, 0).reshape(8, 27 * MID)
    one = one.transpose(1, 2, 0).reshape(4, 54 * CIN)
    return feature, one, two


def solution(mesh):
    split = Mesh(mesh.devices.reshape(4, 2, 2, 4, 4), ("x", "zl", "core", "y", "zh"))
    cells = P(CHAN, SLAB, None, None)
    return jax.shard_map(
        shards,
        mesh=split,
        in_specs=(cells, cells, cells, P(), P(), P(), P()),
        out_specs=(cells, P(CHAN, None), P(CHAN, None)),
        check_vma=False,
    )
```
